256 devices in a mesh: grp: 8 (over x, core), slab: 32 (over y, z).
Axes of the slice: x: 4, y: 4, z: 8, core: 2. Of those that a mesh axis runs over, the one named last changes fastest.
Arguments:
- pre: bfloat16 [128, 128, 64, 128], P('slab', 'grp'), may hold values from -6 to 6
- cotan: bfloat16 [128, 128, 64, 128], P('slab', 'grp'), may hold values from -6 to 6
- pointwise: bfloat16 [64, 64], replicated, may hold values from -0.75 to 0.75
- spectral: bfloat16 [32, 32, 32, 64, 128], P('slab', 'grp'), may hold values from -0.5 to 0.5
- w_in: float32 [6, 512], replicated, may hold values from -2.5 to 2.5
- b_in: float32 [512], replicated, may hold values from -3 to 3
- w_mid: float32 [512, 256], replicated, may hold values from -0.25 to 0.25
- b_mid: float32 [256], replicated, may hold values from -3 to 3
- w_out: float32 [256, 64], replicated, may hold values from -0.375 to 0.375
- b_out: float32 [64], replicated, may hold values from -3 to 3
- kernel_inputs: float32 [6, 262144], P(None, ('grp', 'slab')), may hold values from -1 to 1
- voxel_index: int32 [262144], P(('grp', 'slab')), may hold values from 0 to 8191
- routes: int32 [262144, 1], P(('grp', 'slab')), may hold values from 0 to 255; in each aligned block of 1024 rows (0 to 1023, 1024 to 2047, ...) at most 8 rows name the same one
- targets: int32 [262144], P(('grp', 'slab')), may hold values from 0 to 1023
- counts: int32 [2048], P(('grp', 'slab')), may hold values from 96 to 128
Outputs:
- d_features: float32 [64, 262144], P(None, ('grp', 'slab'))
The draws below stay inside these ranges and needn't reach their ends.
Inputs may be any that keep to these rules, and one draw needn't show every extreme that they name: `voxel_index`: a flat index (first, second, third dimension order) into the block of 128/32 by 128/8 by 128 voxels held by the slot's device. `routes`: devices are numbered grp index times 32 plus slab index; among the slots of one device no more than 8 name one device, padded slots included. `counts`: slots of a block at or beyond its count are padding.
All inputs are finite; a program needn't handle non-finite values.
Results may differ from the reference program's by a relative error of at most 0.00035.
Values sent between devices are 32-bit elements; how exact they have to be, the bound alone decides.
No kernel may reach another device: no remote copies, remote signals or barrier semaphores. Data moves between devices by JAX's collectives and lax.ppermute only.
A program may use at most 64 MiB of HBM per device.

```python
import math
import jax
import jax.numpy as jnp
import numpy as np
from jax import lax

C = 64
NG = 128
MODES = 32
IN = 6
H1 = 512
H2 = 256
SLOTS = 128
BLK = 8
PTS_DEV = 1024
PAIRS_DEV = 1024
CAP = 8
PAIRS = 262144
POINTS = 262144
BLOCKS = 2048
VOX = 8192
N_GRP = 8
N_SLAB = 32
DEVICES = 256


def place_ends(values, own_key, smallest, top_value):
    place = [jax.random.randint(jax.random.fold_in(own_key, axis), (), 0, length) for axis, length in enumerate(values.shape)]
    widest = values.shape.index(max(values.shape))
    neighbour = place[:widest] + [(place[widest] + 1) % values.shape[widest]] + place[widest + 1:]
    return values.at[tuple(place)].set(smallest).at[tuple(neighbour)].set(top_value)


def block_scale(key, shape, shards, low, top_value):
    def one(axis_at, parts):
        draws = jax.random.uniform(jax.random.fold_in(jax.random.fold_in(key, 6), axis_at), (parts,), jnp.float32, low / len(shards), top_value / len(shards))
        return jnp.repeat(jnp.exp(draws), shape[axis_at] // parts).reshape((-1,) + (1,) * (len(shape) - axis_at - 1))

    level = one(*shards[0])
    for cut in shards[1:]:
        level = level * one(*cut)
    return level


def shared_out(key, own, number, rows, amount, top, reach, lean):
    order = jax.random.permutation(key, amount)
    packed, common = shares(amount, rows * top, reach, lean, True), shares(amount, rows * top, reach, lean, False)
    places = jnp.arange(amount)

    def named(sizes, rotation):
        used = int((sizes > 0).sum())
        fixed = max(1, used // 4)
        shifted = fixed + (places - fixed + rotation * (used - fixed)) % max(1, amount - fixed)
        return jnp.zeros((amount,), jnp.int32).at[order[jnp.where(places < fixed, places, shifted)]].set(jnp.asarray(sizes, jnp.int32))

    sizes = jnp.where(number % 4 == 0, named(packed, number // 4), named(common, number - number // 4 - 1))
    mixed = jax.random.permutation(jax.random.fold_in(own, 3), amount)
    source_of, taker = mixed[0:amount // 2 * 2:2], mixed[1:amount // 2 * 2:2]
    margin = jnp.minimum(sizes[source_of] - 1, reach - sizes[taker]) // 2
    margin = jnp.where((source_of == order[0]) | (taker == order[0]) | (sizes[taker] == 0), 0, jnp.maximum(margin, 0))
    shifted = jax.random.randint(jax.random.fold_in(own, 4), (amount // 2,), 0, 1 << 20) % (margin + 1)
    sizes = sizes.at[source_of].add(-shifted).at[taker].add(shifted)
    items = jnp.searchsorted(jnp.cumsum(sizes), jnp.arange(rows * top), side="right").astype(jnp.int32)
    table = items.reshape(top, rows).T
    table = table[jax.random.permutation(jax.random.fold_in(own, 1), rows)]
    rotation = jax.random.randint(jax.random.fold_in(own, 2), (rows, 1), 0, top)
    return jnp.take_along_axis(table, (jnp.arange(top)[None, :] + rotation) % top, axis=1)


def shares(number_of, total, most, slope, full):
    weights = [(1 << 20) // math.isqrt(standing ** slope) + 1 for standing in range(1, number_of + 1)]
    largest = most if full else min(most, max(-(-total // number_of), total * weights[0] // sum(weights)))
    least = 1 if total - largest >= number_of - 1 else 0
    given, spare = [largest] + [least] * (number_of - 1), total - largest - least * (number_of - 1)
    while spare > 0:
        candidates = [i for i in range(1, number_of) if given[i] < largest] or [i for i in range(1, number_of) if given[i] < most]
        pool, left = sum([weights[i] for i in candidates]), spare
        for i in candidates:
            addition = min(most - given[i], max(1, left * weights[i] // pool), spare)
            given[i] = given[i] + addition
            spare = spare - addition
    return np.array(given)


def centred(own_key, extent, spread, reach, cuts=(), held_as=jnp.bfloat16):
    level = block_scale(own_key, extent, cuts, -0.22, 0.18) if cuts else 1.0
    result = jax.random.normal(own_key, extent, jnp.float32) * spread * level
    return jnp.minimum(jnp.maximum(result, -reach), reach).astype(held_as)


def setup_inputs(seed: int = 0) -> dict:
    arg_keys = jax.random.split(jax.random.key(seed), 16)
    pre = centred(arg_keys[0], (NG, NG, C, NG), 1.0, 6.0, ((0, 32), (1, 8)))
    cotan = centred(arg_keys[1], (NG, NG, C, NG), 1.0, 6.0, ((0, 32), (1, 8)))
    pointwise = centred(arg_keys[2], (C, C), C ** -0.5, 0.75)
    spectral = centred(arg_keys[3], (MODES, MODES, MODES, C, 2 * C), (2 * C) ** -0.5, 0.5, ((0, 32), (1, 8)))
    w_in = centred(arg_keys[4], (IN, H1), IN ** -0.5, 2.5, (), jnp.float32)
    b_in = centred(arg_keys[5], (H1,), 0.5, 3.0, (), jnp.float32)
    w_mid = centred(arg_keys[6], (H1, H2), H1 ** -0.5, 0.25, (), jnp.float32)
    b_mid = centred(arg_keys[7], (H2,), 0.5, 3.0, (), jnp.float32)
    w_out = centred(arg_keys[8], (H2, C), H2 ** -0.5, 0.375, (), jnp.float32)
    b_out = centred(arg_keys[9], (C,), 0.5, 3.0, (), jnp.float32)
    kernel_inputs = jnp.clip(jax.random.uniform(arg_keys[10], (IN, PAIRS), jnp.float32, -1.0, 1.0) * block_scale(arg_keys[10], (IN, PAIRS), ((1, 256),), -0.4, 0.0), -1.0, 1.0)
    voxel_index = place_ends(jax.random.randint(arg_keys[11], (PAIRS,), 0, VOX), jax.random.fold_in(arg_keys[11], 1), 0, VOX - 1).astype(jnp.int32)
    routes_keys = jax.random.split(jax.random.fold_in(arg_keys[12], 1), PAIRS // PAIRS_DEV)
    routes_turns = jax.random.permutation(jax.random.fold_in(arg_keys[12], 3), PAIRS // PAIRS_DEV)
    routes = jax.vmap(lambda own, number: shared_out(jax.random.fold_in(arg_keys[12], 2), own, number, PAIRS_DEV, DEVICES, 1, CAP, 2))(routes_keys, routes_turns).reshape((PAIRS, 1))
    targets = place_ends(jax.random.randint(arg_keys[13], (PAIRS,), 0, PTS_DEV), jax.random.fold_in(arg_keys[13], 1), 0, PTS_DEV - 1).astype(jnp.int32)
    counts = place_ends(jax.random.randint(arg_keys[14], (BLOCKS,), 96, 129), jax.random.fold_in(arg_keys[14], 1), 96, 128).astype(jnp.int32)
    return {"pre": pre, "cotan": cotan, "pointwise": pointwise, "spectral": spectral, "w_in": w_in, "b_in": b_in, "w_mid": w_mid, "b_mid": b_mid, "w_out": w_out, "b_out": b_out, "kernel_inputs": kernel_inputs, "voxel_index": voxel_index, "routes": routes, "targets": targets, "counts": counts}


HIGHEST = lax.Precision.HIGHEST

def tables(length, mode_count):
    position = jnp.arange(length, dtype=jnp.int32)
    frequency = jnp.arange(mode_count, dtype=jnp.int32) - mode_count // 2
    product = jnp.mod(position[:, None] * frequency[None, :], length)
    angle = product.astype(jnp.float32) * (2.0 * math.pi / length)
    return (jnp.cos(angle), jnp.sin(angle))

def transform(real_part, imag_part, cos_table, sin_table, form, sign):
    real_cos = jnp.einsum(form, real_part, cos_table, precision=HIGHEST)
    real_sin = jnp.einsum(form, real_part, sin_table, precision=HIGHEST)
    imag_cos = jnp.einsum(form, imag_part, cos_table, precision=HIGHEST)
    imag_sin = jnp.einsum(form, imag_part, sin_table, precision=HIGHEST)
    return (real_cos - sign * imag_sin, imag_cos + sign * real_sin)

def slope_of(values):
    normal_cdf = 0.5 * (1.0 + jax.scipy.special.erf(values / math.sqrt(2.0)))
    return normal_cdf + values * jnp.exp(-0.5 * values * values) / math.sqrt(2.0 * math.pi)

def kernel_values(inputs, w_in, b_in, w_mid, b_mid, w_out, b_out):
    hidden = jax.nn.gelu(jnp.dot(w_in.T, inputs, precision=HIGHEST) + b_in[:, None], approximate=False)
    hidden = jax.nn.gelu(jnp.dot(w_mid.T, hidden, precision=HIGHEST) + b_mid[:, None], approximate=False)
    return jnp.dot(w_out.T, hidden, precision=HIGHEST) + b_out[:, None]

def mix_modes(real_part, imag_part, spectral, channels, scale):
    weights = spectral.astype(jnp.float32)
    real_w = weights[..., :channels]
    imag_w = weights[..., channels:]
    form = 'akod,dakco->akcd'
    mixed_real = (jnp.einsum(form, real_part, real_w, precision=HIGHEST) + jnp.einsum(form, imag_part, imag_w, precision=HIGHEST)) * scale
    mixed_imag = (jnp.einsum(form, imag_part, real_w, precision=HIGHEST) - jnp.einsum(form, real_part, imag_w, precision=HIGHEST)) * scale
    return (mixed_real, mixed_imag)

def reference(pre, cotan, pointwise, spectral, w_in, b_in, w_mid, b_mid, w_out, b_out, kernel_inputs, voxel_index, routes, targets, counts):
    grad_pre = cotan.astype(jnp.float32) * slope_of(pre.astype(jnp.float32))
    cos_table, sin_table = tables(NG, MODES)
    real_part = jnp.einsum('xycz,zk->xyck', grad_pre, cos_table, precision=HIGHEST)
    imag_part = -jnp.einsum('xycz,zk->xyck', grad_pre, sin_table, precision=HIGHEST)
    real_part, imag_part = transform(real_part, imag_part, cos_table, sin_table, 'nycd,nk->kycd', -1.0)
    real_part, imag_part = transform(real_part, imag_part, cos_table, sin_table, 'ancd,nk->akcd', -1.0)
    real_part, imag_part = mix_modes(real_part, imag_part, spectral, C, 1.0 / float(NG) ** 3)
    real_part, imag_part = transform(real_part, imag_part, cos_table, sin_table, 'akcd,nk->ancd', 1.0)
    real_part, imag_part = transform(real_part, imag_part, cos_table, sin_table, 'kycd,nk->nycd', 1.0)
    spectral_part = jnp.einsum('xyck,zk->xycz', real_part, cos_table, precision=HIGHEST) - jnp.einsum('xyck,zk->xycz', imag_part, sin_table, precision=HIGHEST)
    local_part = jnp.einsum('xyod,co->xycd', grad_pre, pointwise.astype(jnp.float32), precision=HIGHEST)
    grad_latent = local_part + spectral_part
    width_x = NG // N_SLAB
    width_y = NG // N_GRP

    def per_device(items):
        index, inputs, voxels, valid_counts = items
        grp_index = index // N_SLAB
        slab_index = index % N_SLAB
        cell_x = slab_index * width_x + voxels // (width_y * NG)
        cell_y = grp_index * width_y + voxels // NG % width_y
        cell_z = voxels % NG
        kernel = kernel_values(inputs, w_in, b_in, w_mid, b_mid, w_out, b_out)
        valid_mask = (jnp.arange(SLOTS, dtype=jnp.int32)[None, :] < valid_counts[:, None]).reshape(-1).astype(jnp.float32)
        return kernel.T * valid_mask[:, None] * grad_latent[cell_x, cell_y, :, cell_z]
    contributions = lax.map(per_device, (jnp.arange(DEVICES, dtype=jnp.int32), kernel_inputs.reshape(IN, DEVICES, PAIRS_DEV).transpose(1, 0, 2), voxel_index.reshape(DEVICES, PAIRS_DEV), counts.reshape(DEVICES, BLK)))
    points = routes[:, 0] * PTS_DEV + targets
    totals = jax.ops.segment_sum(contributions.reshape(-1, C), points, num_segments=POINTS)
    return totals.T
```

```python
import functools
import math

import jax
import jax.numpy as jnp
import numpy as np
from jax import lax
from jax.experimental import pallas as pl
from jax.experimental.pallas import tpu as pltpu
from jax.sharding import PartitionSpec as P

F32 = jnp.float32
BF16 = jnp.bfloat16
NG = 128
MODES = 32
CH = 64
NN = (((1,), (0,)), ((), ()))
NT = (((1,), (1,)), ((), ()))
TN = (((0,), (0,)), ((), ()))


def dot(a, b, dims=NN, precision=None):
    return lax.dot_general(a, b, dims, precision=precision, preferred_element_type=F32)


def tables():
    position = np.arange(NG)
    frequency = np.arange(MODES) - MODES // 2
    angle = (np.outer(frequency, position) % NG) * (2.0 * math.pi / NG)
    parts = []
    for table in (np.cos(angle), np.sin(angle)):
        high = table.astype(np.float32).astype(BF16)
        low = (table - high.astype(np.float64)).astype(np.float32).astype(BF16)
        parts.append((high, low))
    (ch, cl), (sh, sl) = parts
    zero = np.zeros_like(ch)
    forward = np.block([[ch, ch], [sh, sh], [cl, zero], [sl, zero]])
    inverse = np.concatenate([ch.T, ch.T, cl.T, sh.T, sh.T, sl.T], axis=1)
    return forward, inverse


def split(x):
    high = x.astype(BF16)
    return high, (x - high.astype(F32)).astype(BF16)


def lanes_of(shape):
    return lax.broadcasted_iota(jnp.int32, shape, len(shape) - 1)


def swap(x):
    return pltpu.roll(x, 64, 1)


def turn(x):
    return jnp.where(lanes_of(x.shape) < 64, swap(x), -swap(x))


def gelu(x):
    return 0.5 * x * (1.0 + lax.erf(x * (1.0 / math.sqrt(2.0))))


def forward_parts(product, first, width):
    at = slice(first, first + width)
    cos_part = product[0:32, at] + product[64:96, at]
    sin_part = product[32:64, at] + product[96:128, at]
    return cos_part, sin_part


def modes_z_kernel(pre_ref, cotan_ref, table_ref, out_ref, grad_ref):
    step = pl.program_id(0)
    pre = pre_ref[...].astype(F32).reshape(512, 128)
    cotan = cotan_ref[...].astype(F32).reshape(512, 128)
    cdf = 0.5 * (1.0 + lax.erf(pre * (1.0 / math.sqrt(2.0))))
    grad = cotan * (cdf + pre * jnp.exp(-0.5 * pre * pre) * (1.0 / math.sqrt(2.0 * math.pi)))
    high, low = split(grad)
    both = jnp.concatenate([high, low], axis=1)
    grad_ref[...] = both
    product = dot(table_ref[...], both, NT)
    for pair in range(4):
        real, minus = forward_parts(product, pair * 128, 128)
        imag = -minus
        left = lanes_of(real.shape) < 64
        row = step * 8 + 2 * pair
        out_ref[pl.ds(row, 32, stride=64), :] = jnp.where(left, real, swap(imag))
        out_ref[pl.ds(row + 1, 32, stride=64), :] = jnp.where(left, swap(real), imag)


def modes_x_kernel(in_ref, table_ref, out_ref):
    for y in range(0, 16, 2):
        data = jnp.concatenate([in_ref[pl.ds(y + h, 128, stride=16), :] for h in range(2)], axis=1)
        high, low = split(data)
        product = dot(table_ref[...], jnp.concatenate([high, low], axis=0))
        for h in range(2):
            cos_part, sin_part = forward_parts(product, h * 128, 128)
            out_ref[pl.ds(y + h, 32, stride=16), :] = cos_part + turn(sin_part)


def inverse_stack(mixed):
    mixed_high, mixed_low = split(mixed)
    high, low = split(-turn(mixed))
    return jnp.concatenate([mixed_high, mixed_low, mixed_high, high, low, high], axis=0)


def mix_kernel(in_ref, spectral_ref, forward_ref, inverse_ref, out_ref):
    for kx in range(4):
        data = jnp.concatenate(
            [in_ref[g * 64 + kx * 16 : g * 64 + kx * 16 + 16, :] for g in range(8)], axis=0
        )
        high, low = split(data)
        product = dot(forward_ref[...], jnp.concatenate([high, low], axis=0))
        cos_part, sin_part = forward_parts(product, 0, 128)
        hat = cos_part + turn(sin_part)
        other = turn(hat)
        halves = []
        for part in range(2):
            at = slice(part * 16, part * 16 + 16)
            high, low = split(jnp.concatenate([hat[at], other[at]], axis=0))
            first = (kx * 32 + part * 16) * 64
            cross = dot(
                jnp.concatenate([high, low], axis=0), spectral_ref[first : first + 1024, :], NT
            )
            cross = cross[:32] + cross[32:]
            row = lax.broadcasted_iota(jnp.int32, (16, 128), 0)
            real = jnp.zeros((16, 128), F32)
            imag = jnp.zeros((16, 128), F32)
            for pair in range(8):
                own = (row >> 1) == pair
                at = slice(pair * 128, pair * 128 + 128)
                real = jnp.where(own, cross[:16, at], real)
                imag = jnp.where(own, cross[16:, at], imag)
            even = (row & 1) == 0
            left = lanes_of((16, 128)) < 64
            halves.append(
                jnp.where(
                    left,
                    jnp.where(even, real, swap(real)),
                    jnp.where(even, swap(imag), imag),
                )
            )
        mixed = jnp.concatenate(halves, axis=0) * (1.0 / float(NG) ** 3)
        field = dot(inverse_ref[...], inverse_stack(mixed))
        for g in range(8):
            out_ref[g * 64 + kx * 16 : g * 64 + kx * 16 + 16, :] = field[g * 16 : g * 16 + 16]


def field_x_kernel(in_ref, table_ref, out_ref):
    for y in range(0, 16, 2):
        stack = jnp.concatenate(
            [inverse_stack(in_ref[pl.ds(y + h, 32, stride=16), :]) for h in range(2)], axis=1
        )
        field = dot(table_ref[...], stack)
        for h in range(2):
            out_ref[pl.ds(y + h, 128, stride=16), :] = field[:, h * 128 : h * 128 + 128]


def rank_kernel(dest_ref, target_ref, code_ref, send_ref):
    dest = dest_ref[...]
    hit = lax.broadcasted_iota(jnp.int32, (256, 1024), 0) == dest
    one_hot = jnp.where(hit, 1.0, 0.0).astype(BF16)
    earlier = lax.broadcasted_iota(jnp.int32, (1024, 1024), 0) < lanes_of((1024, 1024))
    count = dot(one_hot, jnp.where(earlier, 1.0, 0.0).astype(BF16))
    rank = jnp.sum(jnp.where(hit, count, 0.0), axis=0, keepdims=True).astype(jnp.int32)
    code_ref[...] = (dest * 5 + (rank >> 1)) * 2 + (rank & 1)
    number = target_ref[...] + 1
    own = lax.broadcasted_iota(jnp.int32, (128, 1024), 0) == rank
    coarse = jnp.where(own, ((number >> 5) << 5).astype(F32), 0.0).astype(BF16)
    fine = jnp.where(own, (number & 31).astype(F32), 0.0).astype(BF16)
    send_ref[...] = dot(one_hot, coarse, NT) + dot(one_hot, fine, NT) - 1.0


def kernel_net_kernel(
    in_ref, w_in_ref, w_mid_ref, b_mid_ref, w_out_ref, b_out_ref, counts_ref, out_ref
):
    high = lax.Precision.HIGH
    for block in range(4):
        at = slice(block * 256, block * 256 + 256)
        hidden = gelu(dot(in_ref[:, at], w_in_ref[...], TN, high))
        hidden = gelu(dot(hidden, w_mid_ref[...], NN, high) + b_mid_ref[...])
        value = dot(hidden, w_out_ref[...], NT, high) + b_out_ref[...]
        for part in range(2):
            row = lax.broadcasted_iota(jnp.int32, (128, 128), 0)
            out_ref[block * 256 + part * 128 : block * 256 + part * 128 + 128, :] = jnp.where(
                row < counts_ref[block * 2 + part], value[part * 128 : part * 128 + 128], 0.0
            )


def local_kernel(grad_ref, weight_ref, voxel_ref, out_ref, table_ref):
    def fill(step, carry):
        for part in range(4):
            cell = step * 4 + part
            grad = grad_ref[pl.ds(pl.multiple_of(cell * 64, 64), 64), :]
            stack = jnp.concatenate([grad[:, :128], grad[:, 128:]], axis=0)
            rows = dot(weight_ref[...], stack)
            table_ref[pl.ds(pl.multiple_of(cell * 128, 128), 128), :] = rows.T
        return carry

    lax.fori_loop(0, 16, fill, 0)

    def take(step, carry):
        for part in range(16):
            slot = step * 16 + part
            out_ref[pl.ds(slot, 1), :] = table_ref[pl.ds(voxel_ref[slot], 1), :]
        return carry

    lax.fori_loop(0, 64, take, 0)


def slots_kernel(
    in_ref, table_ref, kernel_ref, local_ref, targets_ref, code_ref, voxel_ref, out_ref, field_ref
):
    out_ref[...] = jnp.zeros_like(out_ref)
    out_ref[pl.ds(4, 256, stride=5), :] = targets_ref[...]

    def fill(step, carry):
        for part in range(4):
            stacks = []
            first = step * 8 + part * 2
            for h in range(2):
                data = in_ref[pl.ds(first + h, 32, stride=64), :]
                other = swap(data)
                left = lanes_of(data.shape) < 64
                real_high, real_low = split(jnp.where(left, data, other))
                imag_high, imag_low = split(-jnp.where(left, other, data))
                stacks.append(
                    jnp.concatenate(
                        [real_high, real_low, real_high, imag_high, imag_low, imag_high], axis=0
                    )
                )
            field = dot(table_ref[...], jnp.concatenate(stacks, axis=1))
            for h in range(2):
                at = pl.multiple_of((first + h) * 128, 128)
                field_ref[pl.ds(at, 128), :] = field[:, h * 128 : h * 128 + 128]
        return carry

    lax.fori_loop(0, 8, fill, 0)
    side = lanes_of((1, 128)) >> 6

    def place(step, carry):
        for part in range(16):
            slot = step * 16 + part
            code = code_ref[slot]
            value = (
                field_ref[pl.ds(voxel_ref[slot], 1), :] + local_ref[pl.ds(slot, 1), :]
            ) * kernel_ref[pl.ds(slot, 1), :]
            pltpu.store(out_ref.at[pl.ds(code >> 1, 1), :], value, mask=side == (code & 1))
        return carry

    lax.fori_loop(0, 64, place, 0)


def gather_kernel(in_ref, out_ref):
    targets = in_ref[pl.ds(4, 256, stride=5), :]
    point = lanes_of((256, 1024)).astype(F32)
    total = jnp.zeros((128, 1024), F32)
    for pair in range(4):
        data = in_ref[pl.ds(pair, 256, stride=5), :].T
        high, low = split(data)
        for h in range(2):
            at = slice(h * 64, h * 64 + 64)
            column = targets[:, pair * 2 + h : pair * 2 + h + 1]
            one_hot = jnp.where(column == point, 1.0, 0.0).astype(BF16)
            total = total + dot(jnp.concatenate([high[at], low[at]], axis=0), one_hot)
    out_ref[...] = total[:64] + total[64:]


VMEM = pl.BlockSpec(memory_space=pltpu.VMEM)
SMEM = pl.BlockSpec(memory_space=pltpu.SMEM)
LIMIT = 48 * 1024 * 1024


def call(body, out_shape, in_specs, scratch=(), **more):
    return pl.pallas_call(
        body,
        out_shape=out_shape,
        in_specs=in_specs,
        scratch_shapes=list(scratch),
        compiler_params=pltpu.CompilerParams(vmem_limit_bytes=LIMIT),
        **more,
    )


def exchange(rows, axis, members):
    count = rows.shape[0] // members
    moved = lax.all_to_all(
        rows.reshape(members, count, 128), axis, split_axis=0, concat_axis=0, tiled=True
    )
    return moved.reshape(rows.shape)


def local(
    pre,
    cotan,
    pointwise,
    spectral,
    w_in,
    b_in,
    w_mid,
    b_mid,
    w_out,
    b_out,
    kernel_inputs,
    voxel_index,
    routes,
    targets,
    counts,
):
    forward, inverse = tables()
    forward, inverse = jnp.asarray(forward), jnp.asarray(inverse)
    shape = jax.ShapeDtypeStruct

    block = pl.BlockSpec((8, 64, 128), lambda i: (i, 0, 0))
    whole = pl.BlockSpec((128, 256), lambda i: (0, 0))
    columns, grad = call(
        modes_z_kernel,
        (shape((2048, 128), F32), shape((4096, 256), BF16)),
        [block, block, whole],
        grid=(8,),
        out_specs=(
            pl.BlockSpec((2048, 128), lambda i: (0, 0)),
            pl.BlockSpec((512, 256), lambda i: (i, 0)),
        ),
    )(pre.reshape(64, 64, 128), cotan.reshape(64, 64, 128), forward)

    routes, targets, kernel_inputs, grad = lax.optimization_barrier(
        (routes, targets, kernel_inputs, grad)
    )
    code, send_targets = call(
        rank_kernel,
        (shape((1, 1024), jnp.int32), shape((256, 128), F32)),
        [VMEM, VMEM],
    )(routes.reshape(1, 1024), targets.reshape(1, 1024))
    code = code.reshape(1024)
    net_in = jnp.concatenate([kernel_inputs, jnp.ones((1, 1024), F32), jnp.zeros((1, 1024), F32)])
    first_layer = jnp.concatenate([w_in, b_in[None], jnp.zeros((1, 512), F32)])
    kernel = call(
        kernel_net_kernel, shape((1024, 128), F32), [VMEM] * 6 + [SMEM]
    )(
        net_in,
        first_layer,
        w_mid,
        b_mid[None],
        jnp.concatenate([w_out.T, w_out.T]),
        jnp.concatenate([b_out, b_out])[None],
        counts,
    )
    weight = jnp.concatenate([pointwise, pointwise], axis=0)
    weight = jnp.concatenate([weight, weight], axis=1)
    own = call(
        local_kernel,
        shape((1024, 128), F32),
        [VMEM, VMEM, SMEM],
        [pltpu.VMEM((8192, 128), F32)],
    )(grad, weight, voxel_index)

    columns = exchange(columns, "slab", 32)
    rows = call(modes_x_kernel, shape((512, 128), F32), [VMEM, VMEM])(columns, forward)
    rows = exchange(rows, "grp", 8)
    rows = call(mix_kernel, shape((512, 128), F32), [VMEM] * 4)(
        rows, spectral.reshape(8192, 128), forward, inverse
    )
    rows = exchange(rows, "grp", 8)
    columns = call(field_x_kernel, shape((2048, 128), F32), [VMEM, VMEM])(rows, inverse)
    columns = exchange(columns, "slab", 32)
    slots = call(
        slots_kernel,
        shape((1280, 128), F32),
        [VMEM] * 5 + [SMEM] * 2,
        [pltpu.VMEM((8192, 128), F32)],
    )(columns, inverse, kernel, own, send_targets, code, voxel_index)
    slots = exchange(slots, ("grp", "slab"), 256)
    return call(gather_kernel, shape((64, 1024), F32), [VMEM])(slots)


def solution(mesh):
    placed = (
        P("slab", "grp", None, None),
        P("slab", "grp", None, None),
        P(),
        P("slab", "grp", None, None, None),
        P(),
        P(),
        P(),
        P(),
        P(),
        P(),
        P(None, ("grp", "slab")),
        P(("grp", "slab")),
        P(("grp", "slab"), None),
        P(("grp", "slab")),
        P(("grp", "slab")),
    )
    return jax.shard_map(
        local, mesh=mesh, in_specs=placed, out_specs=P(None, ("grp", "slab")), check_vma=False
    )
```

```python
import functools
import math

import jax
import jax.numpy as jnp
import numpy as np
from jax import lax
from jax.experimental import pallas as pl
from jax.experimental.pallas import tpu as pltpu
from jax.sharding import PartitionSpec as P

F32 = jnp.float32
BF16 = jnp.bfloat16
NG = 128
MODES = 32
CH = 64
NN = (((1,), (0,)), ((), ()))
NT = (((1,), (1,)), ((), ()))
TN = (((0,), (0,)), ((), ()))


def dot(a, b, dims=NN, precision=None):
    return lax.dot_general(a, b, dims, precision=precision, preferred_element_type=F32)


def tables():
    position = np.arange(NG)
    frequency = np.arange(MODES) - MODES // 2
    angle = (np.outer(frequency, position) % NG) * (2.0 * math.pi / NG)
    parts = []
    for table in (np.cos(angle), np.sin(angle)):
        high = table.astype(np.float32).astype(BF16)
        low = (table - high.astype(np.float64)).astype(np.float32).astype(BF16)
        parts.append((high, low))
    (ch, cl), (sh, sl) = parts
    zero = np.zeros_like(ch)
    forward = np.block([[ch, ch], [sh, sh], [cl, zero], [sl, zero]])
    inverse = np.concatenate([ch.T, ch.T, cl.T, sh.T, sh.T, sl.T], axis=1)
    return forward, inverse


def split(x):
    high = x.astype(BF16)
    return high, (x - high.astype(F32)).astype(BF16)


def lanes_of(shape):
    return lax.broadcasted_iota(jnp.int32, shape, len(shape) - 1)


def swap(x):
    return pltpu.roll(x, 64, 1)


def turn(x):
    return jnp.where(lanes_of(x.shape) < 64, swap(x), -swap(x))


def gelu(x):
    return 0.5 * x * (1.0 + lax.erf(x * (1.0 / math.sqrt(2.0))))


def forward_parts(product, first, width):
    at = slice(first, first + width)
    cos_part = product[0:32, at] + product[64:96, at]
    sin_part = product[32:64, at] + product[96:128, at]
    return cos_part, sin_part


def slope_times(pre, cotan):
    cdf = 0.5 * (1.0 + lax.erf(pre * (1.0 / math.sqrt(2.0))))
    return cotan * (cdf + pre * jnp.exp(-0.5 * pre * pre) * (1.0 / math.sqrt(2.0 * math.pi)))


def rank_slots(dest, target, code_ref, send_ref):
    hit = lax.broadcasted_iota(jnp.int32, (256, 1024), 0) == dest
    one_hot = jnp.where(hit, 1.0, 0.0).astype(BF16)
    lane = lanes_of((128, 256))
    earlier = (lax.broadcasted_iota(jnp.int32, (128, 256), 0) < lane) | (lane >= 128)
    earlier = jnp.where(earlier, 1.0, 0.0).astype(BF16)
    before = jnp.zeros((256, 128), F32)
    ranks = []
    for block in range(8):
        at = slice(block * 128, block * 128 + 128)
        count = dot(one_hot[:, at], earlier)
        own = jnp.where(hit[:, at], count[:, :128] + before, 0.0)
        ranks.append(jnp.sum(own, axis=0, keepdims=True))
        before = before + count[:, 128:]
    rank = jnp.concatenate(ranks, axis=1).astype(jnp.int32)
    code_ref[...] = dest * 8 + rank
    number = target + 1
    group = lax.broadcasted_iota(jnp.int32, (16, 1024), 0) == (dest >> 5)
    group = jnp.where(group, 1.0, 0.0).astype(BF16)
    own = lax.broadcasted_iota(jnp.int32, (256, 1024), 0) == ((dest & 31) * 8 + rank)
    coarse = jnp.where(own, ((number >> 5) << 5).astype(F32), 0.0).astype(BF16)
    fine = jnp.where(own, (number & 31).astype(F32), 0.0).astype(BF16)
    send_ref[...] = (dot(group, coarse, NT) + dot(group, fine, NT))[:8]


def modes_z_kernel(
    pre_hbm,
    cotan_hbm,
    table_hbm,
    dest_hbm,
    target_hbm,
    out_ref,
    code_ref,
    send_ref,
    pre_ref,
    cotan_ref,
    table_ref,
    dest_ref,
    target_ref,
    sems,
    small_sems,
):
    small = (
        pltpu.make_async_copy(dest_hbm, dest_ref, small_sems.at[0]),
        pltpu.make_async_copy(target_hbm, target_ref, small_sems.at[1]),
        pltpu.make_async_copy(table_hbm, table_ref, small_sems.at[2]),
    )
    for copy in small:
        copy.start()
    loads = []
    for step in range(8):
        at = pl.ds(step * 8, 8)
        loads.append(pltpu.make_async_copy(pre_hbm.at[at], pre_ref.at[at], sems.at[step, 0]))
        loads.append(pltpu.make_async_copy(cotan_hbm.at[at], cotan_ref.at[at], sems.at[step, 1]))
    for copy in loads:
        copy.start()
    for copy in small:
        copy.wait()
    rank_slots(dest_ref[...], target_ref[...], code_ref, send_ref)
    for copy in loads:
        copy.wait()
    for step in range(8):
        at = pl.ds(step * 8, 8)
        pre = pre_ref[at].astype(F32).reshape(512, 128)
        cotan = cotan_ref[at].astype(F32).reshape(512, 128)
        high, low = split(slope_times(pre, cotan))
        product = dot(table_ref[...], jnp.concatenate([high, low], axis=1), NT)
        for pair in range(4):
            real, minus = forward_parts(product, pair * 128, 128)
            imag = -minus
            left = lanes_of(real.shape) < 64
            row = step * 8 + 2 * pair
            out_ref[pl.ds(row, 32, stride=64), :] = jnp.where(left, real, swap(imag))
            out_ref[pl.ds(row + 1, 32, stride=64), :] = jnp.where(left, swap(real), imag)


def modes_x_kernel(in_ref, table_ref, out_ref):
    for y in range(0, 16, 2):
        data = jnp.concatenate([in_ref[pl.ds(y + h, 128, stride=16), :] for h in range(2)], axis=1)
        high, low = split(data)
        product = dot(table_ref[...], jnp.concatenate([high, low], axis=0))
        for h in range(2):
            cos_part, sin_part = forward_parts(product, h * 128, 128)
            out_ref[pl.ds(y + h, 32, stride=16), :] = cos_part + turn(sin_part)


def inverse_stack(mixed):
    mixed_high, mixed_low = split(mixed)
    high, low = split(-turn(mixed))
    return jnp.concatenate([mixed_high, mixed_low, mixed_high, high, low, high], axis=0)


def mix_kernel(in_ref, spectral_ref, forward_ref, inverse_ref, targets_ref, out_ref):
    for half in range(2):
        out_ref[pl.ds(64 + half, 8, stride=66), :] = targets_ref[:, half * 128 : half * 128 + 128]
    for kx in range(4):
        data = jnp.concatenate(
            [in_ref[g * 64 + kx * 16 : g * 64 + kx * 16 + 16, :] for g in range(8)], axis=0
        )
        high, low = split(data)
        product = dot(forward_ref[...], jnp.concatenate([high, low], axis=0))
        cos_part, sin_part = forward_parts(product, 0, 128)
        hat = cos_part + turn(sin_part)
        other = turn(hat)
        halves = []
        for part in range(2):
            at = slice(part * 16, part * 16 + 16)
            high, low = split(jnp.concatenate([hat[at], other[at]], axis=0))
            first = (kx * 32 + part * 16) * 64
            cross = dot(
                jnp.concatenate([high, low], axis=0), spectral_ref[first : first + 1024, :], NT
            )
            cross = cross[:32] + cross[32:]
            row = lax.broadcasted_iota(jnp.int32, (16, 128), 0)
            real = jnp.zeros((16, 128), F32)
            imag = jnp.zeros((16, 128), F32)
            for pair in range(8):
                own = (row >> 1) == pair
                at = slice(pair * 128, pair * 128 + 128)
                real = jnp.where(own, cross[:16, at], real)
                imag = jnp.where(own, cross[16:, at], imag)
            even = (row & 1) == 0
            left = lanes_of((16, 128)) < 64
            halves.append(
                jnp.where(
                    left,
                    jnp.where(even, real, swap(real)),
                    jnp.where(even, swap(imag), imag),
                )
            )
        mixed = jnp.concatenate(halves, axis=0) * (1.0 / float(NG) ** 3)
        field = dot(inverse_ref[...], inverse_stack(mixed))
        for g in range(8):
            out_ref[g * 66 + kx * 16 : g * 66 + kx * 16 + 16, :] = field[g * 16 : g * 16 + 16]


def field_x_kernel(in_ref, table_ref, out_ref):
    number = jnp.concatenate(
        [in_ref[pl.ds(64 + half, 8, stride=66), :] for half in range(2)], axis=1
    ).astype(jnp.int32)
    own = (lanes_of((32, 256)) >> 3) == lax.broadcasted_iota(jnp.int32, (32, 256), 0)
    total = jnp.zeros((64, 128), F32)
    for g in range(8):
        row = number[g : g + 1]
        coarse = jnp.where(own, ((row >> 5) << 5).astype(F32), 0.0)
        fine = jnp.where(own, (row & 31).astype(F32), 0.0)
        place = (lax.broadcasted_iota(jnp.int32, (256, 128), 0) & 7) + g * 8
        fold = jnp.where(place == lanes_of((256, 128)), 1.0, 0.0).astype(BF16)
        total = total + dot(jnp.concatenate([coarse, fine], axis=0).astype(BF16), fold)
    out_ref[pl.ds(64, 32, stride=65), :] = total[:32] + total[32:]
    for y in range(0, 16, 2):
        stacks = []
        for h in range(2):
            low = in_ref[pl.ds(y + h, 4, stride=16), :]
            parts = [low] + [in_ref[pl.ds(g * 66 + y + h, 4, stride=16), :] for g in range(1, 8)]
            stacks.append(inverse_stack(jnp.concatenate(parts, axis=0)))
        field = dot(table_ref[...], jnp.concatenate(stacks, axis=1))
        for h in range(2):
            for s in range(32):
                out_ref[pl.ds(s * 65 + y + h, 4, stride=16), :] = field[
                    s * 4 : s * 4 + 4, h * 128 : h * 128 + 128
                ]


def kernel_net_kernel(
    in_ref, w_in_ref, w_mid_ref, b_mid_ref, w_out_ref, b_out_ref, counts_ref, after_hbm, out_ref
):
    del after_hbm
    high = lax.Precision.HIGH
    for block in range(4):
        at = slice(block * 256, block * 256 + 256)
        hidden = gelu(dot(in_ref[:, at], w_in_ref[...], TN, high))
        hidden = gelu(dot(hidden, w_mid_ref[...], NN, high) + b_mid_ref[...])
        value = dot(hidden, w_out_ref[...], NT, high) + b_out_ref[...]
        for part in range(2):
            row = lax.broadcasted_iota(jnp.int32, (128, 128), 0)
            out_ref[block * 256 + part * 128 : block * 256 + part * 128 + 128, :] = jnp.where(
                row < counts_ref[block * 2 + part], value[part * 128 : part * 128 + 128], 0.0
            )


def local_kernel(pre_ref, cotan_ref, weight_ref, voxel_ref, after_hbm, out_ref, table_ref):
    del after_hbm

    def fill(step, carry):
        at = pl.ds(step * 4, 4)
        pre = pre_ref[at].astype(F32).reshape(256, 128)
        cotan = cotan_ref[at].astype(F32).reshape(256, 128)
        high, low = split(slope_times(pre, cotan))
        for part in range(4):
            own = slice(part * 64, part * 64 + 64)
            rows = dot(weight_ref[...], jnp.concatenate([high[own], low[own]], axis=0))
            first = pl.multiple_of((step * 4 + part) * 128, 128)
            table_ref[pl.ds(first, 128), :] = rows.T
        return carry

    lax.fori_loop(0, 16, fill, 0)

    def take(step, carry):
        for part in range(16):
            slot = step * 16 + part
            out_ref[pl.ds(slot, 1), :] = table_ref[pl.ds(voxel_ref[slot], 1), :]
        return carry

    lax.fori_loop(0, 64, take, 0)


def slots_kernel(
    in_ref,
    table_ref,
    kernel_hbm,
    local_hbm,
    code_ref,
    voxel_ref,
    out_ref,
    numbers_ref,
    field_ref,
    kernel_ref,
    local_ref,
    sems,
):
    copies = (
        pltpu.make_async_copy(kernel_hbm, kernel_ref, sems.at[0]),
        pltpu.make_async_copy(local_hbm, local_ref, sems.at[1]),
    )
    for copy in copies:
        copy.start()
    out_ref[...] = jnp.zeros_like(out_ref)
    numbers_ref[...] = in_ref[pl.ds(64, 32, stride=65), :]

    def fill(step, carry):
        for part in range(4):
            stacks = []
            first = step * 8 + part * 2
            for h in range(2):
                data = in_ref[pl.ds(first + h, 32, stride=65), :]
                other = swap(data)
                left = lanes_of(data.shape) < 64
                real_high, real_low = split(jnp.where(left, data, other))
                imag_high, imag_low = split(-jnp.where(left, other, data))
                stacks.append(
                    jnp.concatenate(
                        [real_high, real_low, real_high, imag_high, imag_low, imag_high], axis=0
                    )
                )
            field = dot(table_ref[...], jnp.concatenate(stacks, axis=1))
            for h in range(2):
                at = pl.multiple_of((first + h) * 128, 128)
                field_ref[pl.ds(at, 128), :] = field[:, h * 128 : h * 128 + 128]
        return carry

    lax.fori_loop(0, 8, fill, 0, unroll=2)
    side = lanes_of((1, 128)) >> 6
    for copy in copies:
        copy.wait()

    def place(step, carry):
        for part in range(16):
            slot = step * 16 + part
            code = code_ref[slot]
            value = (
                field_ref[pl.ds(voxel_ref[slot], 1), :] + local_ref[pl.ds(slot, 1), :]
            ) * kernel_ref[pl.ds(slot, 1), :]
            pltpu.store(out_ref.at[pl.ds(code >> 1, 1), :], value, mask=side == (code & 1))
        return carry

    lax.fori_loop(0, 64, place, 0, unroll=2)


def gather_kernel(in_ref, numbers_ref, out_ref):
    numbers = numbers_ref[...] - 1.0
    point = lanes_of((256, 1024)).astype(F32)
    total = jnp.zeros((128, 1024), F32)
    for pair in range(4):
        data = in_ref[pl.ds(pair, 256, stride=4), :].T
        high, low = split(data)
        for h in range(2):
            at = slice(h * 64, h * 64 + 64)
            rank = pair * 2 + h
            column = jnp.concatenate(
                [numbers[:, g * 8 + rank : g * 8 + rank + 1] for g in range(8)], axis=0
            )
            one_hot = jnp.where(column == point, 1.0, 0.0).astype(BF16)
            total = total + dot(jnp.concatenate([high[at], low[at]], axis=0), one_hot)
    out_ref[...] = total[:64] + total[64:]


VMEM = pl.BlockSpec(memory_space=pltpu.VMEM)
SMEM = pl.BlockSpec(memory_space=pltpu.SMEM)
HBM = pl.BlockSpec(memory_space=pltpu.HBM)
ANY = pl.BlockSpec(memory_space=pl.ANY)
LIMIT = 16 * 1024 * 1024


def call(body, out_shape, in_specs, scratch=(), **more):
    return pl.pallas_call(
        body,
        out_shape=out_shape,
        in_specs=in_specs,
        scratch_shapes=list(scratch),
        compiler_params=pltpu.CompilerParams(vmem_limit_bytes=LIMIT),
        **more,
    )


def in_hbm(x):
    return pltpu.with_memory_space_constraint(x, pltpu.HBM)


def exchange(rows, axis, members):
    count = rows.shape[0] // members
    chunks = (members, count, 128) if count % 8 == 0 else (members, 1, count * 128)
    moved = lax.all_to_all(rows.reshape(chunks), axis, split_axis=0, concat_axis=0, tiled=True)
    return moved.reshape(rows.shape)


def local(
    pre,
    cotan,
    pointwise,
    spectral,
    w_in,
    b_in,
    w_mid,
    b_mid,
    w_out,
    b_out,
    kernel_inputs,
    voxel_index,
    routes,
    targets,
    counts,
):
    forward, inverse = tables()
    forward, inverse = jnp.asarray(forward), jnp.asarray(inverse)
    shape = jax.ShapeDtypeStruct
    pre, cotan = pre.reshape(64, 64, 128), cotan.reshape(64, 64, 128)

    columns, code, send_targets = call(
        modes_z_kernel,
        (shape((2048, 128), F32), shape((1, 1024), jnp.int32), shape((8, 256), F32)),
        [HBM] * 5,
        [
            pltpu.VMEM((64, 64, 128), BF16),
            pltpu.VMEM((64, 64, 128), BF16),
            pltpu.VMEM((128, 256), BF16),
            pltpu.VMEM((1, 1024), jnp.int32),
            pltpu.VMEM((1, 1024), jnp.int32),
            pltpu.SemaphoreType.DMA((8, 2)),
            pltpu.SemaphoreType.DMA((3,)),
        ],
    )(
        in_hbm(pre),
        in_hbm(cotan),
        in_hbm(forward),
        in_hbm(routes.reshape(1, 1024)),
        in_hbm(targets.reshape(1, 1024)),
    )
    code = code.reshape(1024)

    columns = exchange(columns, "slab", 32)
    rows = call(modes_x_kernel, shape((512, 128), F32), [VMEM, VMEM])(columns, forward)
    rows = exchange(rows, "grp", 8)
    rows = call(mix_kernel, shape((528, 128), F32), [VMEM] * 5)(
        rows, spectral.reshape(8192, 128), forward, inverse, send_targets
    )
    rows = exchange(rows, "grp", 8)
    columns = call(field_x_kernel, shape((2080, 128), F32), [VMEM, VMEM])(rows, inverse)

    net_in = jnp.concatenate([kernel_inputs, jnp.ones((1, 1024), F32), jnp.zeros((1, 1024), F32)])
    first_layer = jnp.concatenate([w_in, b_in[None], jnp.zeros((1, 512), F32)])
    kernel = call(
        kernel_net_kernel, pltpu.HBM((1024, 128), F32), [VMEM] * 6 + [SMEM, ANY]
    )(
        net_in,
        first_layer,
        w_mid,
        b_mid[None],
        jnp.concatenate([w_out.T, w_out.T]),
        jnp.concatenate([b_out, b_out])[None],
        counts,
        columns,
    )
    weight = jnp.concatenate([pointwise, pointwise], axis=0)
    weight = jnp.concatenate([weight, weight], axis=1)
    own = call(
        local_kernel,
        pltpu.HBM((1024, 128), F32),
        [VMEM, VMEM, VMEM, SMEM, ANY],
        [pltpu.VMEM((8192, 128), F32)],
    )(pre, cotan, weight, voxel_index, columns)

    columns = exchange(columns, "slab", 32)
    slots, numbers = call(
        slots_kernel,
        (shape((1024, 128), F32), shape((32, 128), F32)),
        [VMEM, VMEM, HBM, HBM, SMEM, SMEM],
        [
            pltpu.VMEM((8192, 128), F32),
            pltpu.VMEM((1024, 128), F32),
            pltpu.VMEM((1024, 128), F32),
            pltpu.SemaphoreType.DMA((2,)),
        ],
    )(columns, inverse, in_hbm(kernel), in_hbm(own), code, voxel_index)
    slots = exchange(slots, ("grp", "slab"), 256)
    return call(gather_kernel, shape((64, 1024), F32), [VMEM, VMEM])(slots, numbers)


def solution(mesh):
    placed = (
        P("slab", "grp", None, None),
        P("slab", "grp", None, None),
        P(),
        P("slab", "grp", None, None, None),
        P(),
        P(),
        P(),
        P(),
        P(),
        P(),
        P(None, ("grp", "slab")),
        P(("grp", "slab")),
        P(("grp", "slab"), None),
        P(("grp", "slab")),
        P(("grp", "slab")),
    )
    return jax.shard_map(
        local, mesh=mesh, in_specs=placed, out_specs=P(None, ("grp", "slab")), check_vma=False
    )
```

```python
import functools
import math

import jax
import jax.numpy as jnp
import numpy as np
from jax import lax
from jax.experimental import pallas as pl
from jax.experimental.pallas import tpu as pltpu
from jax.sharding import PartitionSpec as P

F32 = jnp.float32
BF16 = jnp.bfloat16
NG = 128
MODES = 32
CH = 64
NN = (((1,), (0,)), ((), ()))
NT = (((1,), (1,)), ((), ()))
TN = (((0,), (0,)), ((), ()))


def dot(a, b, dims=NN, precision=None):
    return lax.dot_general(a, b, dims, precision=precision, preferred_element_type=F32)


def tables():
    position = np.arange(NG)
    frequency = np.arange(MODES) - MODES // 2
    angle = (np.outer(frequency, position) % NG) * (2.0 * math.pi / NG)
    parts = []
    for table in (np.cos(angle), np.sin(angle)):
        high = table.astype(np.float32).astype(BF16)
        low = (table - high.astype(np.float64)).astype(np.float32).astype(BF16)
        parts.append((high, low))
    (ch, cl), (sh, sl) = parts
    zero = np.zeros_like(ch)
    forward = np.block([[ch, ch], [sh, sh], [cl, zero], [sl, zero]])
    inverse = np.concatenate([ch.T, ch.T, cl.T, sh.T, sh.T, sl.T], axis=1)
    return forward, inverse


def split(x):
    high = x.astype(BF16)
    return high, (x - high.astype(F32)).astype(BF16)


def lanes_of(shape):
    return lax.broadcasted_iota(jnp.int32, shape, len(shape) - 1)


def swap(x):
    return pltpu.roll(x, 64, 1)


def turn(x):
    return jnp.where(lanes_of(x.shape) < 64, swap(x), -swap(x))


def gelu(x):
    return 0.5 * x * (1.0 + lax.erf(x * (1.0 / math.sqrt(2.0))))


def forward_parts(product, first, width):
    at = slice(first, first + width)
    cos_part = product[0:32, at] + product[64:96, at]
    sin_part = product[32:64, at] + product[96:128, at]
    return cos_part, sin_part


def slope_times(pre, cotan):
    cdf = 0.5 * (1.0 + lax.erf(pre * (1.0 / math.sqrt(2.0))))
    return cotan * (cdf + pre * jnp.exp(-0.5 * pre * pre) * (1.0 / math.sqrt(2.0 * math.pi)))


def earlier_same(one_hot, hit):
    lane = lanes_of((128, 256))
    earlier = (lax.broadcasted_iota(jnp.int32, (128, 256), 0) < lane) | (lane >= 128)
    earlier = jnp.where(earlier, 1.0, 0.0).astype(BF16)
    before = jnp.zeros((hit.shape[0], 128), F32)
    ranks = []
    for block in range(8):
        at = slice(block * 128, block * 128 + 128)
        count = dot(one_hot[:, at], earlier)
        own = jnp.where(hit[:, at], count[:, :128] + before, 0.0)
        ranks.append(jnp.sum(own, axis=0, keepdims=True))
        before = before + count[:, 128:]
    return jnp.concatenate(ranks, axis=1).astype(jnp.int32), before


def rank_slots(dest, target, code_ref, send_ref):
    hit = lax.broadcasted_iota(jnp.int32, (256, 1024), 0) == dest
    one_hot = jnp.where(hit, 1.0, 0.0).astype(BF16)
    rank, _ = earlier_same(one_hot, hit)
    code_ref[...] = dest * 8 + rank
    number = target + 1
    group = lax.broadcasted_iota(jnp.int32, (16, 1024), 0) == (dest >> 5)
    group = jnp.where(group, 1.0, 0.0).astype(BF16)
    own = lax.broadcasted_iota(jnp.int32, (256, 1024), 0) == ((dest & 31) * 8 + rank)
    coarse = jnp.where(own, ((number >> 5) << 5).astype(F32), 0.0).astype(BF16)
    fine = jnp.where(own, (number & 31).astype(F32), 0.0).astype(BF16)
    send_ref[...] = (dot(group, coarse, NT) + dot(group, fine, NT))[:8]


def modes_z_kernel(
    pre_hbm,
    cotan_hbm,
    table_hbm,
    dest_hbm,
    target_hbm,
    out_ref,
    code_ref,
    send_ref,
    pre_ref,
    cotan_ref,
    table_ref,
    dest_ref,
    target_ref,
    sems,
    small_sems,
):
    small = (
        pltpu.make_async_copy(dest_hbm, dest_ref, small_sems.at[0]),
        pltpu.make_async_copy(target_hbm, target_ref, small_sems.at[1]),
        pltpu.make_async_copy(table_hbm, table_ref, small_sems.at[2]),
    )
    for copy in small:
        copy.start()
    loads = []
    for step in range(2):
        at = pl.ds(step * 32, 32)
        loads.append(pltpu.make_async_copy(pre_hbm.at[at], pre_ref.at[at], sems.at[step, 0]))
        loads.append(pltpu.make_async_copy(cotan_hbm.at[at], cotan_ref.at[at], sems.at[step, 1]))
    for copy in loads:
        copy.start()
    for copy in small:
        copy.wait()
    for copy in loads:
        copy.wait()
    rank_slots(dest_ref[...], target_ref[...], code_ref, send_ref)
    for step in range(8):
        at = pl.ds(step * 8, 8)
        pre = pre_ref[at].astype(F32).reshape(512, 128)
        cotan = cotan_ref[at].astype(F32).reshape(512, 128)
        high, low = split(slope_times(pre, cotan))
        product = dot(table_ref[...], jnp.concatenate([high, low], axis=1), NT)
        for pair in range(4):
            real, minus = forward_parts(product, pair * 128, 128)
            imag = -minus
            left = lanes_of(real.shape) < 64
            row = step * 8 + 2 * pair
            out_ref[pl.ds(row, 32, stride=64), :] = jnp.where(left, real, swap(imag))
            out_ref[pl.ds(row + 1, 32, stride=64), :] = jnp.where(left, swap(real), imag)


def modes_x_kernel(in_ref, table_ref, out_ref):
    for y in range(0, 16, 2):
        data = jnp.concatenate([in_ref[pl.ds(y + h, 128, stride=16), :] for h in range(2)], axis=1)
        high, low = split(data)
        product = dot(table_ref[...], jnp.concatenate([high, low], axis=0))
        for h in range(2):
            cos_part, sin_part = forward_parts(product, h * 128, 128)
            out_ref[pl.ds(y + h, 32, stride=16), :] = cos_part + turn(sin_part)


def inverse_stack(mixed):
    mixed_high, mixed_low = split(mixed)
    high, low = split(-turn(mixed))
    return jnp.concatenate([mixed_high, mixed_low, mixed_high, high, low, high], axis=0)


def mix_kernel(in_ref, spectral_ref, forward_ref, inverse_ref, targets_ref, out_ref):
    for half in range(2):
        out_ref[pl.ds(64 + half, 8, stride=66), :] = targets_ref[:, half * 128 : half * 128 + 128]
    for kx in range(4):
        data = jnp.concatenate(
            [in_ref[g * 64 + kx * 16 : g * 64 + kx * 16 + 16, :] for g in range(8)], axis=0
        )
        high, low = split(data)
        product = dot(forward_ref[...], jnp.concatenate([high, low], axis=0))
        cos_part, sin_part = forward_parts(product, 0, 128)
        hat = cos_part + turn(sin_part)
        other = turn(hat)
        halves = []
        for part in range(2):
            at = slice(part * 16, part * 16 + 16)
            modes = jnp.concatenate([hat[at], other[at]], axis=0)
            second = (lax.broadcasted_iota(jnp.int32, (32, 128), 0) & 1) == 1
            modes = jnp.concatenate(
                [jnp.where(second, 0.0, modes), jnp.where(second, modes, 0.0)], axis=1
            )
            high, low = split(modes)
            first = (kx * 32 + part * 16) * 64
            weights = spectral_ref[first : first + 1024, :].reshape(8, 2, 64, 128)
            weights = jnp.concatenate([weights[:, 0], weights[:, 1]], axis=2).reshape(512, 256)
            cross = dot(jnp.concatenate([high, low], axis=0), weights, NT)
            cross = cross[:32] + cross[32:]
            row = lax.broadcasted_iota(jnp.int32, (16, 128), 0)
            real = jnp.zeros((16, 128), F32)
            imag = jnp.zeros((16, 128), F32)
            for pair in range(4):
                own = (row >> 2) == pair
                at = slice(pair * 128, pair * 128 + 128)
                real = jnp.where(own, cross[:16, at], real)
                imag = jnp.where(own, cross[16:, at], imag)
            even = (row & 2) == 0
            left = lanes_of((16, 128)) < 64
            halves.append(
                jnp.where(
                    left,
                    jnp.where(even, real, swap(real)),
                    jnp.where(even, swap(imag), imag),
                )
            )
        mixed = jnp.concatenate(halves, axis=0) * (1.0 / float(NG) ** 3)
        field = dot(inverse_ref[...], inverse_stack(mixed))
        for g in range(8):
            out_ref[g * 66 + kx * 16 : g * 66 + kx * 16 + 16, :] = field[g * 16 : g * 16 + 16]


def field_x_kernel(in_ref, table_ref, out_ref):
    number = jnp.concatenate(
        [in_ref[pl.ds(64 + half, 8, stride=66), :] for half in range(2)], axis=1
    ).astype(jnp.int32)
    own = (lanes_of((32, 256)) >> 3) == lax.broadcasted_iota(jnp.int32, (32, 256), 0)
    total = jnp.zeros((64, 128), F32)
    for g in range(8):
        row = number[g : g + 1]
        coarse = jnp.where(own, ((row >> 5) << 5).astype(F32), 0.0)
        fine = jnp.where(own, (row & 31).astype(F32), 0.0)
        place = (lax.broadcasted_iota(jnp.int32, (256, 128), 0) & 7) + g * 8
        fold = jnp.where(place == lanes_of((256, 128)), 1.0, 0.0).astype(BF16)
        total = total + dot(jnp.concatenate([coarse, fine], axis=0).astype(BF16), fold)
    out_ref[pl.ds(64, 32, stride=65), :] = total[:32] + total[32:]
    for y in range(0, 16, 2):
        stacks = []
        for h in range(2):
            low = in_ref[pl.ds(y + h, 4, stride=16), :]
            parts = [low] + [in_ref[pl.ds(g * 66 + y + h, 4, stride=16), :] for g in range(1, 8)]
            stacks.append(inverse_stack(jnp.concatenate(parts, axis=0)))
        field = dot(table_ref[...], jnp.concatenate(stacks, axis=1))
        for h in range(2):
            for s in range(32):
                out_ref[pl.ds(s * 65 + y + h, 4, stride=16), :] = field[
                    s * 4 : s * 4 + 4, h * 128 : h * 128 + 128
                ]


def kernel_net_kernel(
    in_ref, w_in_ref, w_mid_ref, b_mid_ref, w_out_ref, b_out_ref, counts_ref, after_hbm, out_ref
):
    del after_hbm
    high = lax.Precision.HIGH
    for block in range(4):
        at = slice(block * 256, block * 256 + 256)
        hidden = gelu(dot(in_ref[:, at], w_in_ref[...], TN, high))
        hidden = gelu(dot(hidden, w_mid_ref[...], NN, high) + b_mid_ref[...])
        value = dot(hidden, w_out_ref[...], NT, high) + b_out_ref[...]
        for part in range(2):
            row = lax.broadcasted_iota(jnp.int32, (128, 128), 0)
            out_ref[block * 256 + part * 128 : block * 256 + part * 128 + 128, :] = jnp.where(
                row < counts_ref[block * 2 + part], value[part * 128 : part * 128 + 128], 0.0
            )


ROOM = 1280


def order_kernel(code_ref, voxel_ref, after_hbm, place_ref, entry_ref, count_ref):
    del after_hbm
    code, voxel = code_ref[...], voxel_ref[...]
    kind = ((voxel >> 7) & 1) * 2 + (code & 1)
    hit = lax.broadcasted_iota(jnp.int32, (16, 1024), 0) == kind
    number, total = earlier_same(jnp.where(hit, 1.0, 0.0).astype(BF16), hit)
    place_ref[...] = kind * ROOM + number
    entry_ref[...] = ((voxel >> 8) * 128 + (voxel & 127)) * 2048 + (code >> 1)
    own = lax.broadcasted_iota(jnp.int32, (16, 128), 0) == lanes_of((16, 128))
    count_ref[...] = jnp.sum(jnp.where(own, total, 0.0), axis=0, keepdims=True).astype(jnp.int32)


def local_kernel(
    pre_ref,
    cotan_ref,
    weight_ref,
    kernel_ref,
    code_ref,
    voxel_ref,
    place_ref,
    entry_ref,
    count_ref,
    scale_ref,
    shift_ref,
    list_ref,
    table_ref,
):
    scale_ref[...] = jnp.zeros_like(scale_ref)
    shift_ref[...] = jnp.zeros_like(shift_ref)

    def fill(step, carry):
        at = pl.ds(step * 4, 4)
        pre = pre_ref[at].astype(F32).reshape(256, 128)
        cotan = cotan_ref[at].astype(F32).reshape(256, 128)
        high, low = split(slope_times(pre, cotan))
        for part in range(4):
            own = slice(part * 64, part * 64 + 64)
            rows = dot(weight_ref[...], jnp.concatenate([high[own], low[own]], axis=0))
            first = pl.multiple_of((step * 4 + part) * 128, 128)
            table_ref[pl.ds(first, 128), :] = rows.T
        return carry

    lax.fori_loop(0, 16, fill, 0)
    side = lanes_of((1, 128)) >> 6

    def place(step, carry):
        for part in range(16):
            slot = step * 16 + part
            code = code_ref[slot]
            voxel = voxel_ref[slot]
            scale = kernel_ref[pl.ds(slot, 1), :]
            shift = table_ref[pl.ds(voxel, 1), :] * scale
            mask = side == (code & 1)
            at = pl.ds(code >> 1, 1)
            pltpu.store(scale_ref.at[at, :], scale, mask=mask)
            pltpu.store(shift_ref.at[at, :], shift, mask=mask)
            list_ref[place_ref[slot]] = entry_ref[slot]
        return carry

    lax.fori_loop(0, 64, place, 0)
    for kind in range(4):
        for part in range(16):
            list_ref[kind * ROOM + count_ref[kind] + part] = 1024
        list_ref[kind * ROOM + ROOM - 1] = count_ref[kind]


def slots_kernel(
    in_ref,
    table_ref,
    scale_hbm,
    shift_hbm,
    list_hbm,
    out_ref,
    numbers_ref,
    field_ref,
    same_ref,
    other_ref,
    scale_ref,
    shift_ref,
    list_ref,
    sems,
):
    list_copy = pltpu.make_async_copy(list_hbm, list_ref, sems.at[2])
    list_copy.start()
    copies = (
        pltpu.make_async_copy(scale_hbm, scale_ref, sems.at[0]),
        pltpu.make_async_copy(shift_hbm, shift_ref, sems.at[1]),
    )
    for copy in copies:
        copy.start()
    numbers_ref[...] = in_ref[pl.ds(64, 32, stride=65), :]
    same_ref[...] = jnp.zeros_like(same_ref)
    other_ref[...] = jnp.zeros_like(other_ref)

    def fill(step, carry):
        for part in range(4):
            stacks = []
            first = step * 8 + part * 2
            for h in range(2):
                even = in_ref[pl.ds(2 * (first + h), 32, stride=65), :]
                odd = in_ref[pl.ds(2 * (first + h) + 1, 32, stride=65), :]
                left = lanes_of(even.shape) < 64
                real_high, real_low = split(jnp.where(left, even, swap(odd)))
                imag_high, imag_low = split(-jnp.where(left, swap(even), odd))
                stacks.append(
                    jnp.concatenate(
                        [real_high, real_low, real_high, imag_high, imag_low, imag_high], axis=0
                    )
                )
            field = dot(table_ref[...], jnp.concatenate(stacks, axis=1))
            for h in range(2):
                at = pl.multiple_of((first + h) * 128, 128)
                field_ref[pl.ds(at, 128), :] = field[:, h * 128 : h * 128 + 128]
        return carry

    lax.fori_loop(0, 4, fill, 0, unroll=2)
    side = lanes_of((1, 128)) >> 6
    list_copy.wait()
    for kind in range(4):
        into_ref = same_ref if kind in (0, 3) else other_ref
        mask = side == (kind >> 1)

        def take(step, carry, kind=kind, into_ref=into_ref, mask=mask):
            entries = [list_ref[kind * ROOM + step * 16 + part] for part in range(16)]
            rows = [field_ref[pl.ds(entry >> 11, 1), :] for entry in entries]
            for entry, row in zip(entries, rows):
                pltpu.store(into_ref.at[pl.ds(entry & 2047, 1), :], row, mask=mask)
            return carry

        lax.fori_loop(0, (list_ref[kind * ROOM + ROOM - 1] + 15) >> 4, take, 0)
    for copy in copies:
        copy.wait()
    for block in range(8):
        at = slice(block * 128, block * 128 + 128)
        out_ref[at] = (same_ref[at] + swap(other_ref[at])) * scale_ref[at] + shift_ref[at]


def gather_kernel(in_ref, numbers_ref, out_hbm, out_ref, sems):
    numbers = numbers_ref[...] - 1.0
    sides = []
    for pair in range(4):
        high, low = split(in_ref[pl.ds(pair, 256, stride=4), :].T)
        for h in range(2):
            at = slice(h * 64, h * 64 + 64)
            rank = pair * 2 + h
            column = jnp.concatenate(
                [numbers[:, g * 8 + rank : g * 8 + rank + 1] for g in range(8)], axis=0
            )
            sides.append((jnp.concatenate([high[at], low[at]], axis=0), column))
    copies = []
    for half in range(2):
        point = lanes_of((256, 512)).astype(F32) + half * 512.0
        total = jnp.zeros((128, 512), F32)
        for data, column in sides:
            total = total + dot(data, jnp.where(column == point, 1.0, 0.0).astype(BF16))
        at = pl.ds(half * 512, 512)
        out_ref[:, half * 512 : half * 512 + 512] = total[:64] + total[64:]
        copies.append(pltpu.make_async_copy(out_ref.at[:, at], out_hbm.at[:, at], sems.at[half]))
        copies[-1].start()
    for copy in copies:
        copy.wait()


VMEM = pl.BlockSpec(memory_space=pltpu.VMEM)
SMEM = pl.BlockSpec(memory_space=pltpu.SMEM)
HBM = pl.BlockSpec(memory_space=pltpu.HBM)
ANY = pl.BlockSpec(memory_space=pl.ANY)
LIMIT = 16 * 1024 * 1024


def call(body, out_shape, in_specs, scratch=(), **more):
    return pl.pallas_call(
        body,
        out_shape=out_shape,
        in_specs=in_specs,
        scratch_shapes=list(scratch),
        compiler_params=pltpu.CompilerParams(vmem_limit_bytes=LIMIT),
        **more,
    )


def in_hbm(x):
    return pltpu.with_memory_space_constraint(x, pltpu.HBM)


def exchange(rows, axis, members):
    count = rows.shape[0] // members
    chunks = (members, count, 128) if count % 8 == 0 else (members, 1, count * 128)
    moved = lax.all_to_all(rows.reshape(chunks), axis, split_axis=0, concat_axis=0, tiled=True)
    return moved.reshape(rows.shape)


def local(
    pre,
    cotan,
    pointwise,
    spectral,
    w_in,
    b_in,
    w_mid,
    b_mid,
    w_out,
    b_out,
    kernel_inputs,
    voxel_index,
    routes,
    targets,
    counts,
):
    forward, inverse = tables()
    forward, inverse = jnp.asarray(forward), jnp.asarray(inverse)
    shape = jax.ShapeDtypeStruct
    pre, cotan = pre.reshape(64, 64, 128), cotan.reshape(64, 64, 128)

    columns, code, send_targets = call(
        modes_z_kernel,
        (shape((2048, 128), F32), shape((1, 1024), jnp.int32), shape((8, 256), F32)),
        [HBM] * 5,
        [
            pltpu.VMEM((64, 64, 128), BF16),
            pltpu.VMEM((64, 64, 128), BF16),
            pltpu.VMEM((128, 256), BF16),
            pltpu.VMEM((1, 1024), jnp.int32),
            pltpu.VMEM((1, 1024), jnp.int32),
            pltpu.SemaphoreType.DMA((2, 2)),
            pltpu.SemaphoreType.DMA((3,)),
        ],
    )(
        in_hbm(pre),
        in_hbm(cotan),
        in_hbm(forward),
        in_hbm(routes.reshape(1, 1024)),
        in_hbm(targets.reshape(1, 1024)),
    )
    code = code.reshape(1024)

    columns = exchange(columns, "slab", 32)
    rows = call(modes_x_kernel, shape((512, 128), F32), [VMEM, VMEM])(columns, forward)
    rows = exchange(rows, "grp", 8)
    rows = call(mix_kernel, shape((528, 128), F32), [VMEM] * 5)(
        rows, spectral.reshape(8192, 128), forward, inverse, send_targets
    )
    rows = exchange(rows, "grp", 8)
    columns = call(field_x_kernel, shape((2080, 128), F32), [VMEM, VMEM])(rows, inverse)

    net_in = jnp.concatenate([kernel_inputs, jnp.ones((1, 1024), F32), jnp.zeros((1, 1024), F32)])
    first_layer = jnp.concatenate([w_in, b_in[None], jnp.zeros((1, 512), F32)])
    kernel = call(
        kernel_net_kernel, shape((1024, 128), F32), [VMEM] * 6 + [SMEM, ANY]
    )(
        net_in,
        first_layer,
        w_mid,
        b_mid[None],
        jnp.concatenate([w_out.T, w_out.T]),
        jnp.concatenate([b_out, b_out])[None],
        counts,
        columns,
    )
    weight = jnp.concatenate([pointwise, pointwise], axis=0)
    weight = jnp.concatenate([weight, weight], axis=1)
    place, entry, count = call(
        order_kernel,
        (
            shape((1, 1024), jnp.int32),
            shape((1, 1024), jnp.int32),
            shape((1, 128), jnp.int32),
        ),
        [VMEM, VMEM, ANY],
    )(code.reshape(1, 1024), voxel_index.reshape(1, 1024), columns)
    count = count.reshape(128)
    scale, shift, entries = call(
        local_kernel,
        (pltpu.HBM((1024, 128), F32), pltpu.HBM((1024, 128), F32), shape((4 * ROOM,), jnp.int32)),
        [VMEM, VMEM, VMEM, VMEM, SMEM, SMEM, SMEM, SMEM, SMEM],
        [pltpu.VMEM((8192, 128), F32)],
        out_specs=(VMEM, VMEM, SMEM),
    )(
        pre,
        cotan,
        weight,
        kernel,
        code,
        voxel_index,
        place.reshape(1024),
        entry.reshape(1024),
        count,
    )

    columns = exchange(columns, "slab", 32)
    slots, numbers = call(
        slots_kernel,
        (shape((1024, 128), F32), shape((32, 128), F32)),
        [VMEM, VMEM, HBM, HBM, HBM],
        [
            pltpu.VMEM((4096, 128), F32),
            pltpu.VMEM((1032, 128), F32),
            pltpu.VMEM((1032, 128), F32),
            pltpu.VMEM((1024, 128), F32),
            pltpu.VMEM((1024, 128), F32),
            pltpu.SMEM((4 * ROOM,), jnp.int32),
            pltpu.SemaphoreType.DMA((3,)),
        ],
    )(columns, inverse, in_hbm(scale), in_hbm(shift), in_hbm(entries))
    slots = exchange(slots, ("grp", "slab"), 256)
    return call(
        gather_kernel,
        shape((64, 1024), F32),
        [VMEM, VMEM],
        [pltpu.VMEM((64, 1024), F32), pltpu.SemaphoreType.DMA((2,))],
        out_specs=HBM,
    )(slots, numbers)


def solution(mesh):
    placed = (
        P("slab", "grp", None, None),
        P("slab", "grp", None, None),
        P(),
        P("slab", "grp", None, None, None),
        P(),
        P(),
        P(),
        P(),
        P(),
        P(),
        P(None, ("grp", "slab")),
        P(("grp", "slab")),
        P(("grp", "slab"), None),
        P(("grp", "slab")),
        P(("grp", "slab")),
    )
    return jax.shard_map(
        local, mesh=mesh, in_specs=placed, out_specs=P(None, ("grp", "slab")), check_vma=False
    )
```

```python
import functools
import math

import jax
import jax.numpy as jnp
import numpy as np
from jax import lax
from jax.experimental import pallas as pl
from jax.experimental.pallas import tpu as pltpu
from jax.sharding import PartitionSpec as P

F32 = jnp.float32
BF16 = jnp.bfloat16
NG = 128
MODES = 32
CH = 64
OUT_STEP, OUT_FIRST = 31, 15
BACK_STEP, BACK_FIRST = 31, 15
NN = (((1,), (0,)), ((), ()))
NT = (((1,), (1,)), ((), ()))
TN = (((0,), (0,)), ((), ()))


def dot(a, b, dims=NN, precision=None):
    return lax.dot_general(a, b, dims, precision=precision, preferred_element_type=F32)


def back_slab(chunk):
    return (chunk * BACK_STEP + BACK_FIRST) & 31


OUT_SLABS = [(chunk * OUT_STEP + OUT_FIRST) & 31 for chunk in range(32)]
BACK_SLABS = [back_slab(chunk) for chunk in range(32)]
OUT_X = [slab * 4 + part for slab in OUT_SLABS for part in range(4)]
BACK_X = [slab * 4 + part for slab in BACK_SLABS for part in range(4)]


def waves(modes, positions):
    frequency = np.array(modes) - MODES // 2
    angle = (np.outer(frequency, np.array(positions)) % NG) * (2.0 * math.pi / NG)
    parts = []
    for table in (np.cos(angle), np.sin(angle)):
        high = table.astype(np.float32).astype(BF16)
        low = (table - high.astype(np.float64)).astype(np.float32).astype(BF16)
        parts.append((high, low))
    return parts


def forward_table(modes, positions):
    (ch, cl), (sh, sl) = waves(modes, positions)
    zero = np.zeros_like(ch)
    return jnp.asarray(np.block([[ch, ch], [sh, sh], [cl, zero], [sl, zero]]))


def inverse_table(modes, positions):
    (ch, cl), (sh, sl) = waves(modes, positions)
    return jnp.asarray(np.concatenate([ch.T, ch.T, cl.T, sh.T, sh.T, sl.T], axis=1))


def split(x):
    high = x.astype(BF16)
    return high, (x - high.astype(F32)).astype(BF16)


def lanes_of(shape):
    return lax.broadcasted_iota(jnp.int32, shape, len(shape) - 1)


def swap(x):
    return pltpu.roll(x, 64, 1)


def turn(x):
    return jnp.where(lanes_of(x.shape) < 64, swap(x), -swap(x))


def gelu(x):
    return 0.5 * x * (1.0 + lax.erf(x * (1.0 / math.sqrt(2.0))))


def forward_parts(product, first, width):
    at = slice(first, first + width)
    cos_part = product[0:32, at] + product[64:96, at]
    sin_part = product[32:64, at] + product[96:128, at]
    return cos_part, sin_part


def slope_times(pre, cotan):
    cdf = 0.5 * (1.0 + lax.erf(pre * (1.0 / math.sqrt(2.0))))
    return cotan * (cdf + pre * jnp.exp(-0.5 * pre * pre) * (1.0 / math.sqrt(2.0 * math.pi)))


def earlier_same(one_hot, hit):
    lane = lanes_of((128, 256))
    earlier = (lax.broadcasted_iota(jnp.int32, (128, 256), 0) < lane) | (lane >= 128)
    earlier = jnp.where(earlier, 1.0, 0.0).astype(BF16)
    before = jnp.zeros((hit.shape[0], 128), F32)
    ranks = []
    for block in range(8):
        at = slice(block * 128, block * 128 + 128)
        count = dot(one_hot[:, at], earlier)
        own = jnp.where(hit[:, at], count[:, :128] + before, 0.0)
        ranks.append(jnp.sum(own, axis=0, keepdims=True))
        before = before + count[:, 128:]
    return jnp.concatenate(ranks, axis=1).astype(jnp.int32), before


def rank_slots(dest, target, code_ref, send_ref):
    hit = lax.broadcasted_iota(jnp.int32, (256, 1024), 0) == dest
    one_hot = jnp.where(hit, 1.0, 0.0).astype(BF16)
    rank, _ = earlier_same(one_hot, hit)
    code_ref[...] = dest * 8 + rank
    number = target + 1
    group = lax.broadcasted_iota(jnp.int32, (16, 1024), 0) == (dest >> 5)
    group = jnp.where(group, 1.0, 0.0).astype(BF16)
    own = lax.broadcasted_iota(jnp.int32, (256, 1024), 0) == ((dest & 31) * 8 + rank)
    coarse = jnp.where(own, ((number >> 5) << 5).astype(F32), 0.0).astype(BF16)
    fine = jnp.where(own, (number & 31).astype(F32), 0.0).astype(BF16)
    send_ref[...] = (dot(group, coarse, NT) + dot(group, fine, NT))[:8]


def modes_z_kernel(
    pre_hbm,
    cotan_hbm,
    table_hbm,
    dest_hbm,
    target_hbm,
    out_ref,
    code_ref,
    send_ref,
    pre_ref,
    cotan_ref,
    table_ref,
    dest_ref,
    target_ref,
    sems,
    small_sems,
):
    small = (
        pltpu.make_async_copy(dest_hbm, dest_ref, small_sems.at[0]),
        pltpu.make_async_copy(target_hbm, target_ref, small_sems.at[1]),
        pltpu.make_async_copy(table_hbm, table_ref, small_sems.at[2]),
    )
    for copy in small:
        copy.start()
    loads = []
    for step in range(2):
        at = pl.ds(step * 32, 32)
        loads.append(pltpu.make_async_copy(pre_hbm.at[at], pre_ref.at[at], sems.at[step, 0]))
        loads.append(pltpu.make_async_copy(cotan_hbm.at[at], cotan_ref.at[at], sems.at[step, 1]))
    for copy in loads:
        copy.start()
    for copy in small:
        copy.wait()
    for copy in loads:
        copy.wait()
    rank_slots(dest_ref[...], target_ref[...], code_ref, send_ref)
    for step in range(8):
        at = pl.ds(step * 8, 8)
        pre = pre_ref[at].astype(F32).reshape(512, 128)
        cotan = cotan_ref[at].astype(F32).reshape(512, 128)
        high, low = split(slope_times(pre, cotan))
        product = dot(table_ref[...], jnp.concatenate([high, low], axis=1), NT)
        for pair in range(4):
            real, minus = forward_parts(product, pair * 128, 128)
            imag = -minus
            left = lanes_of(real.shape) < 64
            row = step * 8 + 2 * pair
            out_ref[pl.ds(row, 32, stride=64), :] = jnp.where(left, real, swap(imag))
            out_ref[pl.ds(row + 1, 32, stride=64), :] = jnp.where(left, swap(real), imag)


def modes_x_kernel(in_ref, table_ref, out_ref):
    for y in range(0, 16, 2):
        data = jnp.concatenate([in_ref[pl.ds(y + h, 128, stride=16), :] for h in range(2)], axis=1)
        high, low = split(data)
        product = dot(table_ref[...], jnp.concatenate([high, low], axis=0))
        for h in range(2):
            cos_part, sin_part = forward_parts(product, h * 128, 128)
            out_ref[pl.ds(y + h, 32, stride=16), :] = cos_part + turn(sin_part)


def inverse_stack(mixed):
    mixed_high, mixed_low = split(mixed)
    high, low = split(-turn(mixed))
    return jnp.concatenate([mixed_high, mixed_low, mixed_high, high, low, high], axis=0)


def mix_kernel(in_ref, spectral_ref, forward_ref, inverse_ref, targets_ref, out_ref):
    for half in range(2):
        out_ref[pl.ds(64 + half, 8, stride=66), :] = targets_ref[:, half * 128 : half * 128 + 128]
    data = jnp.concatenate(
        [
            jnp.concatenate(
                [in_ref[g * 64 + kx * 16 : g * 64 + kx * 16 + 16, :] for g in range(8)], axis=0
            )
            for kx in range(4)
        ],
        axis=1,
    )
    high, low = split(data)
    product = dot(forward_ref[...], jnp.concatenate([high, low], axis=0))
    row = lax.broadcasted_iota(jnp.int32, (16, 128), 0)
    left = lanes_of((16, 128)) < 64
    even = (row & 2) == 0
    second = (lax.broadcasted_iota(jnp.int32, (32, 128), 0) & 1) == 1
    crosses = []
    for kx in range(4):
        cos_part, sin_part = forward_parts(product, kx * 128, 128)
        hat = cos_part + turn(sin_part)
        other = turn(hat)
        for part in range(2):
            at = slice(part * 16, part * 16 + 16)
            modes = jnp.concatenate([hat[at], other[at]], axis=0)
            modes = jnp.concatenate(
                [jnp.where(second, 0.0, modes), jnp.where(second, modes, 0.0)], axis=1
            )
            high, low = split(modes)
            first = (kx * 32 + part * 16) * 64
            weights = spectral_ref[first : first + 1024, :].reshape(8, 2, 64, 128)
            weights = jnp.concatenate([weights[:, 0], weights[:, 1]], axis=2).reshape(512, 256)
            crosses.append(dot(jnp.concatenate([high, low], axis=0), weights, NT))
    stacks = []
    for kx in range(4):
        halves = []
        for part in range(2):
            cross = crosses[kx * 2 + part]
            cross = cross[:32] + cross[32:]
            real = cross[:16, 0:128]
            imag = cross[16:, 0:128]
            for pair in range(1, 4):
                own = (row >> 2) == pair
                at = slice(pair * 128, pair * 128 + 128)
                real = jnp.where(own, cross[:16, at], real)
                imag = jnp.where(own, cross[16:, at], imag)
            halves.append(
                jnp.where(
                    left,
                    jnp.where(even, real, swap(real)),
                    jnp.where(even, swap(imag), imag),
                )
            )
        stacks.append(inverse_stack(jnp.concatenate(halves, axis=0) * (1.0 / float(NG) ** 3)))
    field = dot(inverse_ref[...], jnp.concatenate(stacks, axis=1))
    for kx in range(4):
        for g in range(8):
            out_ref[g * 66 + kx * 16 : g * 66 + kx * 16 + 16, :] = field[
                g * 16 : g * 16 + 16, kx * 128 : kx * 128 + 128
            ]


def field_x_kernel(in_ref, table_ref, out_ref):
    number = jnp.concatenate(
        [in_ref[pl.ds(64 + half, 8, stride=66), :] for half in range(2)], axis=1
    ).astype(jnp.int32)
    slab = back_slab(lax.broadcasted_iota(jnp.int32, (32, 256), 0))
    own = (lanes_of((32, 256)) >> 3) == slab
    total = jnp.zeros((64, 128), F32)
    for g in range(8):
        row = number[g : g + 1]
        coarse = jnp.where(own, ((row >> 5) << 5).astype(F32), 0.0)
        fine = jnp.where(own, (row & 31).astype(F32), 0.0)
        place = (lax.broadcasted_iota(jnp.int32, (256, 128), 0) & 7) + g * 8
        fold = jnp.where(place == lanes_of((256, 128)), 1.0, 0.0).astype(BF16)
        total = total + dot(jnp.concatenate([coarse, fine], axis=0).astype(BF16), fold)
    out_ref[pl.ds(64, 32, stride=65), :] = total[:32] + total[32:]
    for y in range(0, 16, 2):
        stacks = []
        for h in range(2):
            parts = [in_ref[pl.ds(g * 66 + y + h, 4, stride=16), :] for g in range(8)]
            stacks.append(inverse_stack(jnp.concatenate(parts, axis=0)))
        field = dot(table_ref[...], jnp.concatenate(stacks, axis=1))
        for h in range(2):
            for s in range(32):
                out_ref[pl.ds(s * 65 + y + h, 4, stride=16), :] = field[
                    s * 4 : s * 4 + 4, h * 128 : h * 128 + 128
                ]


def kernel_net_kernel(
    in_ref, w_in_ref, w_mid_ref, b_mid_ref, w_out_ref, b_out_ref, counts_ref, after_hbm, out_ref
):
    del after_hbm
    high = lax.Precision.HIGH
    for block in range(4):
        at = slice(block * 256, block * 256 + 256)
        hidden = gelu(dot(in_ref[:, at], w_in_ref[...], TN, high))
        hidden = gelu(dot(hidden, w_mid_ref[...], NN, high) + b_mid_ref[...])
        value = dot(hidden, w_out_ref[...], NT, high) + b_out_ref[...]
        for part in range(2):
            row = lax.broadcasted_iota(jnp.int32, (128, 128), 0)
            out_ref[block * 256 + part * 128 : block * 256 + part * 128 + 128, :] = jnp.where(
                row < counts_ref[block * 2 + part], value[part * 128 : part * 128 + 128], 0.0
            )


ROOM = 1280


def order_kernel(code_ref, voxel_ref, after_hbm, place_ref, entry_ref, count_ref):
    del after_hbm
    code, voxel = code_ref[...], voxel_ref[...]
    kind = ((voxel >> 7) & 1) * 2 + (code & 1)
    hit = lax.broadcasted_iota(jnp.int32, (16, 1024), 0) == kind
    number, total = earlier_same(jnp.where(hit, 1.0, 0.0).astype(BF16), hit)
    place_ref[...] = kind * ROOM + number
    entry_ref[...] = ((voxel >> 8) * 128 + (voxel & 127)) * 2048 + (code >> 1)
    own = lax.broadcasted_iota(jnp.int32, (16, 128), 0) == lanes_of((16, 128))
    count_ref[...] = jnp.sum(jnp.where(own, total, 0.0), axis=0, keepdims=True).astype(jnp.int32)


def local_kernel(
    pre_ref,
    cotan_ref,
    weight_ref,
    kernel_ref,
    code_ref,
    voxel_ref,
    place_ref,
    entry_ref,
    count_ref,
    scale_ref,
    shift_ref,
    list_ref,
    table_ref,
):
    scale_ref[...] = jnp.zeros_like(scale_ref)
    shift_ref[...] = jnp.zeros_like(shift_ref)

    def fill(step, carry):
        at = pl.ds(step * 4, 4)
        pre = pre_ref[at].astype(F32).reshape(256, 128)
        cotan = cotan_ref[at].astype(F32).reshape(256, 128)
        high, low = split(slope_times(pre, cotan))
        for part in range(4):
            own = slice(part * 64, part * 64 + 64)
            rows = dot(weight_ref[...], jnp.concatenate([high[own], low[own]], axis=0))
            first = pl.multiple_of((step * 4 + part) * 128, 128)
            table_ref[pl.ds(first, 128), :] = rows.T
        return carry

    lax.fori_loop(0, 16, fill, 0)
    side = lanes_of((1, 128)) >> 6

    def place(step, carry):
        for part in range(16):
            slot = step * 16 + part
            code = code_ref[slot]
            voxel = voxel_ref[slot]
            scale = kernel_ref[pl.ds(slot, 1), :]
            shift = table_ref[pl.ds(voxel, 1), :] * scale
            mask = side == (code & 1)
            at = pl.ds(code >> 1, 1)
            pltpu.store(scale_ref.at[at, :], scale, mask=mask)
            pltpu.store(shift_ref.at[at, :], shift, mask=mask)
            list_ref[place_ref[slot]] = entry_ref[slot]
        return carry

    lax.fori_loop(0, 64, place, 0)
    for kind in range(4):
        for part in range(16):
            list_ref[kind * ROOM + count_ref[kind] + part] = 1024
        list_ref[kind * ROOM + ROOM - 1] = count_ref[kind]


def slots_kernel(
    in_ref,
    table_ref,
    scale_hbm,
    shift_hbm,
    list_hbm,
    out_ref,
    numbers_ref,
    field_ref,
    same_ref,
    other_ref,
    scale_ref,
    shift_ref,
    list_ref,
    sems,
):
    list_copy = pltpu.make_async_copy(list_hbm, list_ref, sems.at[2])
    list_copy.start()
    copies = (
        pltpu.make_async_copy(scale_hbm, scale_ref, sems.at[0]),
        pltpu.make_async_copy(shift_hbm, shift_ref, sems.at[1]),
    )
    for copy in copies:
        copy.start()
    for row in range(32):
        chunk = BACK_SLABS.index(row)
        numbers_ref[row : row + 1, :] = in_ref[chunk * 65 + 64 : chunk * 65 + 65, :]
    same_ref[...] = jnp.zeros_like(same_ref)
    other_ref[...] = jnp.zeros_like(other_ref)

    def fill(step, carry):
        for part in range(4):
            stacks = []
            first = step * 8 + part * 2
            for h in range(2):
                even = in_ref[pl.ds(2 * (first + h), 32, stride=65), :]
                odd = in_ref[pl.ds(2 * (first + h) + 1, 32, stride=65), :]
                left = lanes_of(even.shape) < 64
                real_high, real_low = split(jnp.where(left, even, swap(odd)))
                imag_high, imag_low = split(-jnp.where(left, swap(even), odd))
                stacks.append(
                    jnp.concatenate(
                        [real_high, real_low, real_high, imag_high, imag_low, imag_high], axis=0
                    )
                )
            field = dot(table_ref[...], jnp.concatenate(stacks, axis=1))
            for h in range(2):
                at = pl.multiple_of((first + h) * 128, 128)
                field_ref[pl.ds(at, 128), :] = field[:, h * 128 : h * 128 + 128]
        return carry

    lax.fori_loop(0, 4, fill, 0, unroll=2)
    side = lanes_of((1, 128)) >> 6
    list_copy.wait()
    for kind in range(4):
        into_ref = same_ref if kind in (0, 3) else other_ref
        mask = side == (kind >> 1)

        def take(step, carry, kind=kind, into_ref=into_ref, mask=mask):
            entries = [list_ref[kind * ROOM + step * 16 + part] for part in range(16)]
            rows = [field_ref[pl.ds(entry >> 11, 1), :] for entry in entries]
            for entry, row in zip(entries, rows):
                pltpu.store(into_ref.at[pl.ds(entry & 2047, 1), :], row, mask=mask)
            return carry

        lax.fori_loop(0, (list_ref[kind * ROOM + ROOM - 1] + 15) >> 4, take, 0)
    for copy in copies:
        copy.wait()
    for block in range(8):
        at = slice(block * 128, block * 128 + 128)
        out_ref[at] = (same_ref[at] + swap(other_ref[at])) * scale_ref[at] + shift_ref[at]


def gather_kernel(in_ref, numbers_ref, out_hbm, out_ref, sems):
    numbers = numbers_ref[...] - 1.0
    sides = []
    for pair in range(4):
        high, low = split(in_ref[pl.ds(pair, 256, stride=4), :].T)
        for h in range(2):
            at = slice(h * 64, h * 64 + 64)
            rank = pair * 2 + h
            column = jnp.concatenate(
                [numbers[:, g * 8 + rank : g * 8 + rank + 1] for g in range(8)], axis=0
            )
            sides.append((jnp.concatenate([high[at], low[at]], axis=0), column))
    copies = []
    for half in range(2):
        point = lanes_of((256, 512)).astype(F32) + half * 512.0
        total = jnp.zeros((128, 512), F32)
        for data, column in sides:
            total = total + dot(data, jnp.where(column == point, 1.0, 0.0).astype(BF16))
        at = pl.ds(half * 512, 512)
        out_ref[:, half * 512 : half * 512 + 512] = total[:64] + total[64:]
        copies.append(pltpu.make_async_copy(out_ref.at[:, at], out_hbm.at[:, at], sems.at[half]))
        copies[-1].start()
    for copy in copies:
        copy.wait()


VMEM = pl.BlockSpec(memory_space=pltpu.VMEM)
SMEM = pl.BlockSpec(memory_space=pltpu.SMEM)
HBM = pl.BlockSpec(memory_space=pltpu.HBM)
ANY = pl.BlockSpec(memory_space=pl.ANY)
LIMIT = 16 * 1024 * 1024


def call(body, out_shape, in_specs, scratch=(), **more):
    return pl.pallas_call(
        body,
        out_shape=out_shape,
        in_specs=in_specs,
        scratch_shapes=list(scratch),
        compiler_params=pltpu.CompilerParams(vmem_limit_bytes=LIMIT),
        **more,
    )


def in_hbm(x):
    return pltpu.with_memory_space_constraint(x, pltpu.HBM)


def exchange(rows, axis, members, order=None):
    count = rows.shape[0] // members
    chunks = (members, count, 128) if count % 8 == 0 else (members, 1, count * 128)
    moved = lax.all_to_all(
        rows.reshape(chunks),
        axis,
        split_axis=0,
        concat_axis=0,
        tiled=True,
        axis_index_groups=None if order is None else [order],
    )
    return moved.reshape(rows.shape)


def local(
    pre,
    cotan,
    pointwise,
    spectral,
    w_in,
    b_in,
    w_mid,
    b_mid,
    w_out,
    b_out,
    kernel_inputs,
    voxel_index,
    routes,
    targets,
    counts,
):
    modes, cells = list(range(MODES)), list(range(NG))
    shape = jax.ShapeDtypeStruct
    pre, cotan = pre.reshape(64, 64, 128), cotan.reshape(64, 64, 128)

    columns, code, send_targets = call(
        modes_z_kernel,
        (shape((2048, 128), F32), shape((1, 1024), jnp.int32), shape((8, 256), F32)),
        [HBM] * 5,
        [
            pltpu.VMEM((64, 64, 128), BF16),
            pltpu.VMEM((64, 64, 128), BF16),
            pltpu.VMEM((128, 256), BF16),
            pltpu.VMEM((1, 1024), jnp.int32),
            pltpu.VMEM((1, 1024), jnp.int32),
            pltpu.SemaphoreType.DMA((2, 2)),
            pltpu.SemaphoreType.DMA((3,)),
        ],
    )(
        in_hbm(pre),
        in_hbm(cotan),
        in_hbm(forward_table(OUT_SLABS, cells)),
        in_hbm(routes.reshape(1, 1024)),
        in_hbm(targets.reshape(1, 1024)),
    )
    code = code.reshape(1024)

    columns = exchange(columns, "slab", 32, OUT_SLABS)
    rows = call(modes_x_kernel, shape((512, 128), F32), [VMEM, VMEM])(columns, forward_table(modes, OUT_X))
    rows = exchange(rows, "grp", 8)
    rows = call(mix_kernel, shape((528, 128), F32), [VMEM] * 5)(
        rows,
        spectral.reshape(8192, 128),
        forward_table(modes, cells),
        inverse_table(modes, cells),
        send_targets,
    )
    rows = exchange(rows, "grp", 8)
    columns = call(field_x_kernel, shape((2080, 128), F32), [VMEM, VMEM])(
        rows, inverse_table(modes, BACK_X)
    )

    net_in = jnp.concatenate([kernel_inputs, jnp.ones((1, 1024), F32), jnp.zeros((1, 1024), F32)])
    first_layer = jnp.concatenate([w_in, b_in[None], jnp.zeros((1, 512), F32)])
    kernel = call(
        kernel_net_kernel, shape((1024, 128), F32), [VMEM] * 6 + [SMEM, ANY]
    )(
        net_in,
        first_layer,
        w_mid,
        b_mid[None],
        jnp.concatenate([w_out.T, w_out.T]),
        jnp.concatenate([b_out, b_out])[None],
        counts,
        columns,
    )
    weight = jnp.concatenate([pointwise, pointwise], axis=0)
    weight = jnp.concatenate([weight, weight], axis=1)
    place, entry, count = call(
        order_kernel,
        (
            shape((1, 1024), jnp.int32),
            shape((1, 1024), jnp.int32),
            shape((1, 128), jnp.int32),
        ),
        [VMEM, VMEM, ANY],
    )(code.reshape(1, 1024), voxel_index.reshape(1, 1024), columns)
    count = count.reshape(128)
    scale, shift, entries = call(
        local_kernel,
        (pltpu.HBM((1024, 128), F32), pltpu.HBM((1024, 128), F32), shape((4 * ROOM,), jnp.int32)),
        [VMEM, VMEM, VMEM, VMEM, SMEM, SMEM, SMEM, SMEM, SMEM],
        [pltpu.VMEM((8192, 128), F32)],
        out_specs=(VMEM, VMEM, SMEM),
    )(
        pre,
        cotan,
        weight,
        kernel,
        code,
        voxel_index,
        place.reshape(1024),
        entry.reshape(1024),
        count,
    )

    columns = exchange(columns, "slab", 32, BACK_SLABS)
    slots, numbers = call(
        slots_kernel,
        (shape((1024, 128), F32), shape((32, 128), F32)),
        [VMEM, VMEM, HBM, HBM, HBM],
        [
            pltpu.VMEM((4096, 128), F32),
            pltpu.VMEM((1032, 128), F32),
            pltpu.VMEM((1032, 128), F32),
            pltpu.VMEM((1024, 128), F32),
            pltpu.VMEM((1024, 128), F32),
            pltpu.SMEM((4 * ROOM,), jnp.int32),
            pltpu.SemaphoreType.DMA((3,)),
        ],
    )(columns, inverse_table(BACK_SLABS, cells), in_hbm(scale), in_hbm(shift), in_hbm(entries))
    slots = exchange(slots, ("grp", "slab"), 256)
    return call(
        gather_kernel,
        shape((64, 1024), F32),
        [VMEM, VMEM],
        [pltpu.VMEM((64, 1024), F32), pltpu.SemaphoreType.DMA((2,))],
        out_specs=HBM,
    )(slots, numbers)


def solution(mesh):
    placed = (
        P("slab", "grp", None, None),
        P("slab", "grp", None, None),
        P(),
        P("slab", "grp", None, None, None),
        P(),
        P(),
        P(),
        P(),
        P(),
        P(),
        P(None, ("grp", "slab")),
        P(("grp", "slab")),
        P(("grp", "slab"), None),
        P(("grp", "slab")),
        P(("grp", "slab")),
    )
    return jax.shard_map(
        local, mesh=mesh, in_specs=placed, out_specs=P(None, ("grp", "slab")), check_vma=False
    )
```

```python
import functools
import math

import jax
import jax.numpy as jnp
import numpy as np
from jax import lax
from jax.experimental import pallas as pl
from jax.experimental.pallas import tpu as pltpu
from jax.sharding import PartitionSpec as P

F32 = jnp.float32
BF16 = jnp.bfloat16
NG = 128
MODES = 32
CH = 64
OUT_STEP, OUT_FIRST = 31, 23
BACK_STEP, BACK_FIRST = 31, 15
NN = (((1,), (0,)), ((), ()))
NT = (((1,), (1,)), ((), ()))
TN = (((0,), (0,)), ((), ()))


def dot(a, b, dims=NN, precision=None):
    return lax.dot_general(a, b, dims, precision=precision, preferred_element_type=F32)


def back_slab(chunk):
    return (chunk * BACK_STEP + BACK_FIRST) & 31


OUT_SLABS = [(chunk * OUT_STEP + OUT_FIRST) & 31 for chunk in range(32)]
BACK_SLABS = [back_slab(chunk) for chunk in range(32)]
OUT_X = [slab * 4 + part for slab in OUT_SLABS for part in range(4)]
BACK_X = [slab * 4 + part for slab in BACK_SLABS for part in range(4)]


def waves(modes, positions):
    frequency = np.array(modes) - MODES // 2
    angle = (np.outer(frequency, np.array(positions)) % NG) * (2.0 * math.pi / NG)
    parts = []
    for table in (np.cos(angle), np.sin(angle)):
        high = table.astype(np.float32).astype(BF16)
        low = (table - high.astype(np.float64)).astype(np.float32).astype(BF16)
        parts.append((high, low))
    return parts


def forward_table(modes, positions):
    (ch, cl), (sh, sl) = waves(modes, positions)
    zero = np.zeros_like(ch)
    return jnp.asarray(np.block([[ch, ch], [sh, sh], [cl, zero], [sl, zero]]))


def inverse_table(modes, positions):
    (ch, cl), (sh, sl) = waves(modes, positions)
    return jnp.asarray(np.concatenate([ch.T, ch.T, cl.T, sh.T, sh.T, sl.T], axis=1))


def split(x):
    high = x.astype(BF16)
    return high, (x - high.astype(F32)).astype(BF16)


def lanes_of(shape):
    return lax.broadcasted_iota(jnp.int32, shape, len(shape) - 1)


def swap(x):
    return pltpu.roll(x, 64, 1)


def turn(x):
    return jnp.where(lanes_of(x.shape) < 64, swap(x), -swap(x))


def gelu(x):
    return 0.5 * x * (1.0 + lax.erf(x * (1.0 / math.sqrt(2.0))))


def forward_parts(product, first, width):
    at = slice(first, first + width)
    cos_part = product[0:32, at] + product[64:96, at]
    sin_part = product[32:64, at] + product[96:128, at]
    return cos_part, sin_part


def slope_times(pre, cotan):
    cdf = 0.5 * (1.0 + lax.erf(pre * (1.0 / math.sqrt(2.0))))
    return cotan * (cdf + pre * jnp.exp(-0.5 * pre * pre) * (1.0 / math.sqrt(2.0 * math.pi)))


def earlier_same(one_hot, hit):
    lane = lanes_of((128, 256))
    earlier = (lax.broadcasted_iota(jnp.int32, (128, 256), 0) < lane) | (lane >= 128)
    earlier = jnp.where(earlier, 1.0, 0.0).astype(BF16)
    before = jnp.zeros((hit.shape[0], 128), F32)
    ranks = []
    for block in range(8):
        at = slice(block * 128, block * 128 + 128)
        count = dot(one_hot[:, at], earlier)
        own = jnp.where(hit[:, at], count[:, :128] + before, 0.0)
        ranks.append(jnp.sum(own, axis=0, keepdims=True))
        before = before + count[:, 128:]
    return jnp.concatenate(ranks, axis=1).astype(jnp.int32), before


def rank_slots(dest, target, code_ref, send_ref):
    hit = lax.broadcasted_iota(jnp.int32, (256, 1024), 0) == dest
    one_hot = jnp.where(hit, 1.0, 0.0).astype(BF16)
    rank, _ = earlier_same(one_hot, hit)
    code_ref[...] = dest * 8 + rank
    number = target + 1
    group = lax.broadcasted_iota(jnp.int32, (16, 1024), 0) == (dest >> 5)
    group = jnp.where(group, 1.0, 0.0).astype(BF16)
    own = lax.broadcasted_iota(jnp.int32, (256, 1024), 0) == ((dest & 31) * 8 + rank)
    coarse = jnp.where(own, ((number >> 5) << 5).astype(F32), 0.0).astype(BF16)
    fine = jnp.where(own, (number & 31).astype(F32), 0.0).astype(BF16)
    send_ref[...] = (dot(group, coarse, NT) + dot(group, fine, NT))[:8]


def modes_z_kernel(
    pre_hbm,
    cotan_hbm,
    table_hbm,
    dest_hbm,
    target_hbm,
    out_ref,
    code_ref,
    send_ref,
    pre_ref,
    cotan_ref,
    table_ref,
    dest_ref,
    target_ref,
    sems,
    small_sems,
):
    small = (
        pltpu.make_async_copy(dest_hbm, dest_ref, small_sems.at[0]),
        pltpu.make_async_copy(target_hbm, target_ref, small_sems.at[1]),
        pltpu.make_async_copy(table_hbm, table_ref, small_sems.at[2]),
    )
    for copy in small:
        copy.start()
    loads = []
    for step in range(2):
        at = pl.ds(step * 32, 32)
        loads.append(pltpu.make_async_copy(pre_hbm.at[at], pre_ref.at[at], sems.at[step, 0]))
        loads.append(pltpu.make_async_copy(cotan_hbm.at[at], cotan_ref.at[at], sems.at[step, 1]))
    for copy in loads:
        copy.start()
    for copy in small:
        copy.wait()
    for copy in loads:
        copy.wait()
    rank_slots(dest_ref[...], target_ref[...], code_ref, send_ref)
    for step in range(8):
        at = pl.ds(step * 8, 8)
        pre = pre_ref[at].astype(F32).reshape(512, 128)
        cotan = cotan_ref[at].astype(F32).reshape(512, 128)
        high, low = split(slope_times(pre, cotan))
        product = dot(table_ref[...], jnp.concatenate([high, low], axis=1), NT)
        for pair in range(4):
            real, minus = forward_parts(product, pair * 128, 128)
            imag = -minus
            left = lanes_of(real.shape) < 64
            row = step * 8 + 2 * pair
            out_ref[pl.ds(row, 32, stride=64), :] = jnp.where(left, real, swap(imag))
            out_ref[pl.ds(row + 1, 32, stride=64), :] = jnp.where(left, swap(real), imag)


def modes_x_kernel(in_ref, table_ref, out_ref):
    for y in range(0, 16, 2):
        data = jnp.concatenate([in_ref[pl.ds(y + h, 128, stride=16), :] for h in range(2)], axis=1)
        high, low = split(data)
        product = dot(table_ref[...], jnp.concatenate([high, low], axis=0))
        for h in range(2):
            cos_part, sin_part = forward_parts(product, h * 128, 128)
            out_ref[pl.ds(y + h, 32, stride=16), :] = cos_part + turn(sin_part)


def inverse_stack(mixed):
    mixed_high, mixed_low = split(mixed)
    high, low = split(-turn(mixed))
    return jnp.concatenate([mixed_high, mixed_low, mixed_high, high, low, high], axis=0)


def mix_kernel(in_ref, spectral_ref, forward_ref, inverse_ref, targets_ref, out_ref):
    for half in range(2):
        out_ref[pl.ds(64 + half, 8, stride=66), :] = targets_ref[:, half * 128 : half * 128 + 128]
    data = jnp.concatenate(
        [
            jnp.concatenate(
                [in_ref[g * 64 + kx * 16 : g * 64 + kx * 16 + 16, :] for g in range(8)], axis=0
            )
            for kx in range(4)
        ],
        axis=1,
    )
    high, low = split(data)
    product = dot(forward_ref[...], jnp.concatenate([high, low], axis=0))
    row = lax.broadcasted_iota(jnp.int32, (16, 128), 0)
    left = lanes_of((16, 128)) < 64
    even = (row & 2) == 0
    second = (lax.broadcasted_iota(jnp.int32, (32, 128), 0) & 1) == 1
    crosses = []
    for kx in range(4):
        cos_part, sin_part = forward_parts(product, kx * 128, 128)
        hat = cos_part + turn(sin_part)
        other = turn(hat)
        for part in range(2):
            at = slice(part * 16, part * 16 + 16)
            modes = jnp.concatenate([hat[at], other[at]], axis=0)
            modes = jnp.concatenate(
                [jnp.where(second, 0.0, modes), jnp.where(second, modes, 0.0)], axis=1
            )
            high, low = split(modes)
            first = (kx * 32 + part * 16) * 64
            weights = spectral_ref[first : first + 1024, :].reshape(8, 2, 64, 128)
            weights = jnp.concatenate([weights[:, 0], weights[:, 1]], axis=2).reshape(512, 256)
            crosses.append(dot(jnp.concatenate([high, low], axis=0), weights, NT))
    stacks = []
    for kx in range(4):
        halves = []
        for part in range(2):
            cross = crosses[kx * 2 + part]
            cross = cross[:32] + cross[32:]
            real = cross[:16, 0:128]
            imag = cross[16:, 0:128]
            for pair in range(1, 4):
                own = (row >> 2) == pair
                at = slice(pair * 128, pair * 128 + 128)
                real = jnp.where(own, cross[:16, at], real)
                imag = jnp.where(own, cross[16:, at], imag)
            halves.append(
                jnp.where(
                    left,
                    jnp.where(even, real, swap(real)),
                    jnp.where(even, swap(imag), imag),
                )
            )
        stacks.append(inverse_stack(jnp.concatenate(halves, axis=0) * (1.0 / float(NG) ** 3)))
    field = dot(inverse_ref[...], jnp.concatenate(stacks, axis=1))
    for kx in range(4):
        for g in range(8):
            out_ref[g * 66 + kx * 16 : g * 66 + kx * 16 + 16, :] = field[
                g * 16 : g * 16 + 16, kx * 128 : kx * 128 + 128
            ]


def field_x_kernel(in_ref, table_ref, out_ref):
    number = jnp.concatenate(
        [in_ref[pl.ds(64 + half, 8, stride=66), :] for half in range(2)], axis=1
    ).astype(jnp.int32)
    slab = back_slab(lax.broadcasted_iota(jnp.int32, (32, 256), 0))
    own = (lanes_of((32, 256)) >> 3) == slab
    total = jnp.zeros((64, 128), F32)
    for g in range(8):
        row = number[g : g + 1]
        coarse = jnp.where(own, ((row >> 5) << 5).astype(F32), 0.0)
        fine = jnp.where(own, (row & 31).astype(F32), 0.0)
        place = (lax.broadcasted_iota(jnp.int32, (256, 128), 0) & 7) + g * 8
        fold = jnp.where(place == lanes_of((256, 128)), 1.0, 0.0).astype(BF16)
        total = total + dot(jnp.concatenate([coarse, fine], axis=0).astype(BF16), fold)
    out_ref[pl.ds(64, 32, stride=65), :] = total[:32] + total[32:]
    for y in range(0, 16, 2):
        stacks = []
        for h in range(2):
            parts = [in_ref[pl.ds(g * 66 + y + h, 4, stride=16), :] for g in range(8)]
            stacks.append(inverse_stack(jnp.concatenate(parts, axis=0)))
        field = dot(table_ref[...], jnp.concatenate(stacks, axis=1))
        for h in range(2):
            for s in range(32):
                out_ref[pl.ds(s * 65 + y + h, 4, stride=16), :] = field[
                    s * 4 : s * 4 + 4, h * 128 : h * 128 + 128
                ]


def kernel_net_kernel(
    in_ref, w_in_ref, w_mid_ref, b_mid_ref, w_out_ref, b_out_ref, counts_ref, after_hbm, out_ref
):
    del after_hbm
    high = lax.Precision.HIGH
    for block in range(4):
        at = slice(block * 256, block * 256 + 256)
        hidden = gelu(dot(in_ref[:, at], w_in_ref[...], TN, high))
        hidden = gelu(dot(hidden, w_mid_ref[...], NN, high) + b_mid_ref[...])
        value = dot(hidden, w_out_ref[...], NT, high) + b_out_ref[...]
        for part in range(2):
            row = lax.broadcasted_iota(jnp.int32, (128, 128), 0)
            out_ref[block * 256 + part * 128 : block * 256 + part * 128 + 128, :] = jnp.where(
                row < counts_ref[block * 2 + part], value[part * 128 : part * 128 + 128], 0.0
            )


ROOM = 1280


def order_kernel(code_ref, voxel_ref, after_hbm, place_ref, entry_ref, count_ref):
    del after_hbm
    code, voxel = code_ref[...], voxel_ref[...]
    kind = ((voxel >> 7) & 1) * 2 + (code & 1)
    hit = lax.broadcasted_iota(jnp.int32, (16, 1024), 0) == kind
    number, total = earlier_same(jnp.where(hit, 1.0, 0.0).astype(BF16), hit)
    place_ref[...] = kind * ROOM + number
    entry_ref[...] = ((voxel >> 8) * 128 + (voxel & 127)) * 2048 + (code >> 1)
    own = lax.broadcasted_iota(jnp.int32, (16, 128), 0) == lanes_of((16, 128))
    count_ref[...] = jnp.sum(jnp.where(own, total, 0.0), axis=0, keepdims=True).astype(jnp.int32)


def local_kernel(
    pre_ref,
    cotan_ref,
    weight_ref,
    kernel_ref,
    code_ref,
    voxel_ref,
    place_ref,
    entry_ref,
    count_ref,
    scale_ref,
    shift_ref,
    list_ref,
    table_ref,
):
    scale_ref[...] = jnp.zeros_like(scale_ref)
    shift_ref[...] = jnp.zeros_like(shift_ref)

    def fill(step, carry):
        at = pl.ds(step * 4, 4)
        pre = pre_ref[at].astype(F32).reshape(256, 128)
        cotan = cotan_ref[at].astype(F32).reshape(256, 128)
        high, low = split(slope_times(pre, cotan))
        for part in range(4):
            own = slice(part * 64, part * 64 + 64)
            rows = dot(weight_ref[...], jnp.concatenate([high[own], low[own]], axis=0))
            first = pl.multiple_of((step * 4 + part) * 128, 128)
            table_ref[pl.ds(first, 128), :] = rows.T
        return carry

    lax.fori_loop(0, 16, fill, 0)
    side = lanes_of((1, 128)) >> 6

    def place(step, carry):
        for part in range(16):
            slot = step * 16 + part
            code = code_ref[slot]
            voxel = voxel_ref[slot]
            scale = kernel_ref[pl.ds(slot, 1), :]
            shift = table_ref[pl.ds(voxel, 1), :] * scale
            mask = side == (code & 1)
            at = pl.ds(code >> 1, 1)
            pltpu.store(scale_ref.at[at, :], scale, mask=mask)
            pltpu.store(shift_ref.at[at, :], shift, mask=mask)
            list_ref[place_ref[slot]] = entry_ref[slot]
        return carry

    lax.fori_loop(0, 64, place, 0)
    for kind in range(4):
        for part in range(16):
            list_ref[kind * ROOM + count_ref[kind] + part] = 1024
        list_ref[kind * ROOM + ROOM - 1] = count_ref[kind]


def slots_kernel(
    in_ref,
    table_ref,
    scale_hbm,
    shift_hbm,
    list_hbm,
    out_ref,
    numbers_ref,
    field_ref,
    same_ref,
    other_ref,
    scale_ref,
    shift_ref,
    list_ref,
    sems,
):
    list_copy = pltpu.make_async_copy(list_hbm, list_ref, sems.at[2])
    list_copy.start()
    copies = (
        pltpu.make_async_copy(scale_hbm, scale_ref, sems.at[0]),
        pltpu.make_async_copy(shift_hbm, shift_ref, sems.at[1]),
    )
    for copy in copies:
        copy.start()
    for row in range(32):
        chunk = BACK_SLABS.index(row)
        numbers_ref[row : row + 1, :] = in_ref[chunk * 65 + 64 : chunk * 65 + 65, :]
    same_ref[...] = jnp.zeros_like(same_ref)
    other_ref[...] = jnp.zeros_like(other_ref)

    def fill(step, carry):
        for part in range(4):
            stacks = []
            first = step * 8 + part * 2
            for h in range(2):
                even = in_ref[pl.ds(2 * (first + h), 32, stride=65), :]
                odd = in_ref[pl.ds(2 * (first + h) + 1, 32, stride=65), :]
                left = lanes_of(even.shape) < 64
                real_high, real_low = split(jnp.where(left, even, swap(odd)))
                imag_high, imag_low = split(-jnp.where(left, swap(even), odd))
                stacks.append(
                    jnp.concatenate(
                        [real_high, real_low, real_high, imag_high, imag_low, imag_high], axis=0
                    )
                )
            field = dot(table_ref[...], jnp.concatenate(stacks, axis=1))
            for h in range(2):
                at = pl.multiple_of((first + h) * 128, 128)
                field_ref[pl.ds(at, 128), :] = field[:, h * 128 : h * 128 + 128]
        return carry

    lax.fori_loop(0, 4, fill, 0, unroll=2)
    side = lanes_of((1, 128)) >> 6
    list_copy.wait()
    for kind in range(4):
        into_ref = same_ref if kind in (0, 3) else other_ref
        mask = side == (kind >> 1)

        def take(step, carry, kind=kind, into_ref=into_ref, mask=mask):
            entries = [list_ref[kind * ROOM + step * 16 + part] for part in range(16)]
            rows = [field_ref[pl.ds(entry >> 11, 1), :] for entry in entries]
            for entry, row in zip(entries, rows):
                pltpu.store(into_ref.at[pl.ds(entry & 2047, 1), :], row, mask=mask)
            return carry

        lax.fori_loop(0, (list_ref[kind * ROOM + ROOM - 1] + 15) >> 4, take, 0)
    for copy in copies:
        copy.wait()
    for block in range(8):
        at = slice(block * 128, block * 128 + 128)
        out_ref[at] = (same_ref[at] + swap(other_ref[at])) * scale_ref[at] + shift_ref[at]


def gather_kernel(in_ref, numbers_ref, out_hbm, out_ref, sems):
    numbers = numbers_ref[...] - 1.0
    sides = []
    for pair in range(4):
        high, low = split(in_ref[pl.ds(pair, 256, stride=4), :].T)
        for h in range(2):
            at = slice(h * 64, h * 64 + 64)
            rank = pair * 2 + h
            column = jnp.concatenate(
                [numbers[:, g * 8 + rank : g * 8 + rank + 1] for g in range(8)], axis=0
            )
            sides.append((jnp.concatenate([high[at], low[at]], axis=0), column))
    copies = []
    for half in range(2):
        point = lanes_of((256, 512)).astype(F32) + half * 512.0
        total = jnp.zeros((128, 512), F32)
        for data, column in sides:
            total = total + dot(data, jnp.where(column == point, 1.0, 0.0).astype(BF16))
        at = pl.ds(half * 512, 512)
        out_ref[:, half * 512 : half * 512 + 512] = total[:64] + total[64:]
        copies.append(pltpu.make_async_copy(out_ref.at[:, at], out_hbm.at[:, at], sems.at[half]))
        copies[-1].start()
    for copy in copies:
        copy.wait()


VMEM = pl.BlockSpec(memory_space=pltpu.VMEM)
SMEM = pl.BlockSpec(memory_space=pltpu.SMEM)
HBM = pl.BlockSpec(memory_space=pltpu.HBM)
ANY = pl.BlockSpec(memory_space=pl.ANY)
LIMIT = 16 * 1024 * 1024


def call(body, out_shape, in_specs, scratch=(), **more):
    return pl.pallas_call(
        body,
        out_shape=out_shape,
        in_specs=in_specs,
        scratch_shapes=list(scratch),
        compiler_params=pltpu.CompilerParams(vmem_limit_bytes=LIMIT),
        **more,
    )


def in_hbm(x):
    return pltpu.with_memory_space_constraint(x, pltpu.HBM)


def exchange(rows, axis, members, order=None):
    count = rows.shape[0] // members
    chunks = (members, count, 128) if count % 8 == 0 else (members, 1, count * 128)
    moved = lax.all_to_all(
        rows.reshape(chunks),
        axis,
        split_axis=0,
        concat_axis=0,
        tiled=True,
        axis_index_groups=None if order is None else [order],
    )
    return moved.reshape(rows.shape)


def local(
    pre,
    cotan,
    pointwise,
    spectral,
    w_in,
    b_in,
    w_mid,
    b_mid,
    w_out,
    b_out,
    kernel_inputs,
    voxel_index,
    routes,
    targets,
    counts,
):
    modes, cells = list(range(MODES)), list(range(NG))
    shape = jax.ShapeDtypeStruct
    pre, cotan = pre.reshape(64, 64, 128), cotan.reshape(64, 64, 128)

    columns, code, send_targets = call(
        modes_z_kernel,
        (shape((2048, 128), F32), shape((1, 1024), jnp.int32), shape((8, 256), F32)),
        [HBM] * 5,
        [
            pltpu.VMEM((64, 64, 128), BF16),
            pltpu.VMEM((64, 64, 128), BF16),
            pltpu.VMEM((128, 256), BF16),
            pltpu.VMEM((1, 1024), jnp.int32),
            pltpu.VMEM((1, 1024), jnp.int32),
            pltpu.SemaphoreType.DMA((2, 2)),
            pltpu.SemaphoreType.DMA((3,)),
        ],
    )(
        in_hbm(pre),
        in_hbm(cotan),
        in_hbm(forward_table(OUT_SLABS, cells)),
        in_hbm(routes.reshape(1, 1024)),
        in_hbm(targets.reshape(1, 1024)),
    )
    code = code.reshape(1024)

    columns = exchange(columns, "slab", 32, OUT_SLABS)
    rows = call(modes_x_kernel, shape((512, 128), F32), [VMEM, VMEM])(columns, forward_table(modes, OUT_X))
    rows = exchange(rows, "grp", 8)
    rows = call(mix_kernel, shape((528, 128), F32), [VMEM] * 5)(
        rows,
        spectral.reshape(8192, 128),
        forward_table(modes, cells),
        inverse_table(modes, cells),
        send_targets,
    )
    rows = exchange(rows, "grp", 8)
    columns = call(field_x_kernel, shape((2080, 128), F32), [VMEM, VMEM])(
        rows, inverse_table(modes, BACK_X)
    )

    net_in = jnp.concatenate([kernel_inputs, jnp.ones((1, 1024), F32), jnp.zeros((1, 1024), F32)])
    first_layer = jnp.concatenate([w_in, b_in[None], jnp.zeros((1, 512), F32)])
    kernel = call(
        kernel_net_kernel, shape((1024, 128), F32), [VMEM] * 6 + [SMEM, ANY]
    )(
        net_in,
        first_layer,
        w_mid,
        b_mid[None],
        jnp.concatenate([w_out.T, w_out.T]),
        jnp.concatenate([b_out, b_out])[None],
        counts,
        columns,
    )
    weight = jnp.concatenate([pointwise, pointwise], axis=0)
    weight = jnp.concatenate([weight, weight], axis=1)
    place, entry, count = call(
        order_kernel,
        (
            shape((1, 1024), jnp.int32),
            shape((1, 1024), jnp.int32),
            shape((1, 128), jnp.int32),
        ),
        [VMEM, VMEM, ANY],
    )(code.reshape(1, 1024), voxel_index.reshape(1, 1024), columns)
    count = count.reshape(128)
    scale, shift, entries = call(
        local_kernel,
        (pltpu.HBM((1024, 128), F32), pltpu.HBM((1024, 128), F32), shape((4 * ROOM,), jnp.int32)),
        [VMEM, VMEM, VMEM, VMEM, SMEM, SMEM, SMEM, SMEM, SMEM],
        [pltpu.VMEM((8192, 128), F32)],
        out_specs=(VMEM, VMEM, SMEM),
    )(
        pre,
        cotan,
        weight,
        kernel,
        code,
        voxel_index,
        place.reshape(1024),
        entry.reshape(1024),
        count,
    )

    columns = exchange(columns, "slab", 32, BACK_SLABS)
    slots, numbers = call(
        slots_kernel,
        (shape((1024, 128), F32), shape((32, 128), F32)),
        [VMEM, VMEM, HBM, HBM, HBM],
        [
            pltpu.VMEM((4096, 128), F32),
            pltpu.VMEM((1032, 128), F32),
            pltpu.VMEM((1032, 128), F32),
            pltpu.VMEM((1024, 128), F32),
            pltpu.VMEM((1024, 128), F32),
            pltpu.SMEM((4 * ROOM,), jnp.int32),
            pltpu.SemaphoreType.DMA((3,)),
        ],
    )(columns, inverse_table(BACK_SLABS, cells), in_hbm(scale), in_hbm(shift), in_hbm(entries))
    slots = exchange(slots, ("grp", "slab"), 256)
    return call(
        gather_kernel,
        shape((64, 1024), F32),
        [VMEM, VMEM],
        [pltpu.VMEM((64, 1024), F32), pltpu.SemaphoreType.DMA((2,))],
        out_specs=HBM,
    )(slots, numbers)


def solution(mesh):
    placed = (
        P("slab", "grp", None, None),
        P("slab", "grp", None, None),
        P(),
        P("slab", "grp", None, None, None),
        P(),
        P(),
        P(),
        P(),
        P(),
        P(),
        P(None, ("grp", "slab")),
        P(("grp", "slab")),
        P(("grp", "slab"), None),
        P(("grp", "slab")),
        P(("grp", "slab")),
    )
    return jax.shard_map(
        local, mesh=mesh, in_specs=placed, out_specs=P(None, ("grp", "slab")), check_vma=False
    )
```
